256 devices in a mesh: seq: 128 (over y_lo, x, z, core), tp: 2 (over y_hi).
Axes of the slice: x: 4, y: 4 (y_hi: 2, y_lo: 2; y = y_hi * 2 + y_lo), z: 8, core: 2. Of those that a mesh axis runs over, the one named last changes fastest.
Arguments:
- response_query: bfloat16 [128, 512, 5120], P('seq', None, 'tp')
- response_kv: bfloat16 [128, 512, 2, 1024], P('seq', None, None, 'tp'), may hold values from -6 to 6
- prompt_cache: bfloat16 [128, 16, 2, 1024], P('seq', 'tp')
- prompt_order: int32 [16], replicated, may hold values from 0 to 15, each once
- response_prompt: int32 [128], P('seq'), may hold values from 0 to 15
- response_length: int32 [128], P('seq'), may hold values from 1 to 512, 32768 in all
- out_grad: bfloat16 [128, 512, 5120], P('seq', None, 'tp'), may hold values from -6 to 6
Outputs:
- attention_out: bfloat16 [128, 512, 5120], P('seq', None, 'tp')
- query_grad: bfloat16 [128, 512, 5120], P('seq', None, 'tp')
- response_kv_grad: bfloat16 [128, 512, 2, 1024], P('seq', None, None, 'tp')
- prompt_cache_grad: bfloat16 [128, 16, 2, 1024], P('seq', 'tp')
The draws below stay inside these ranges and needn't reach their ends.
Inputs may be any that keep to these rules, and one draw needn't show every extreme that they name: prompt_order names each of the 16 prompts once. `response_length`: some response has all 512 tokens live.
All inputs are finite; a program needn't handle non-finite values. No bound on the sum of `response_length` on one device may be relied on, other than what follows from the above.
Results may differ from the reference program's by a relative error of at most 0.0065.
Values may be sent and summed in bfloat16 or wider, within the bound.
A program may use at most 128 MiB of HBM per device.

```python
import math
import jax
import jax.numpy as jnp
import numpy as np
from jax import lax

HQ = 40
KVH = 8
HD = 128
PLEN = 128
RMAX = 512
PROMPTS = 16
RESP = 128


def draw_response_query(key, part):
    key = jax.random.fold_in(key, 11)
    base = jax.random.normal(key, (RESP, RMAX, HQ, HD), jnp.float32)
    return base.reshape(RESP, RMAX, HQ * HD).astype(jnp.bfloat16)


def draw_prompt_cache(key, part):
    key = jax.random.fold_in(key, 23)
    base = jax.random.normal(key, (PLEN, PROMPTS, 2, KVH, HD), jnp.float32)
    return base.reshape(PLEN, PROMPTS, 2, KVH * HD).astype(jnp.bfloat16)


def with_ends(array, stream_key, low, largest):
    extent = array.shape
    spot = [jax.random.randint(jax.random.fold_in(stream_key, axis), (), 0, extent[axis]) for axis in range(len(extent))]
    array = array.at[tuple(spot)].set(low)
    longest = extent.index(max(extent))
    spot[longest] = (spot[longest] + 1) % extent[longest]
    return array.at[tuple(spot)].set(largest)


def block_levels(stream_key, shape, shards, low, high):
    def one(axis_at, parts):
        steps = jax.random.uniform(jax.random.fold_in(jax.random.fold_in(stream_key, 6), axis_at), (parts,), jnp.float32, low / len(shards), high / len(shards))
        return jnp.repeat(jnp.exp(steps), shape[axis_at] // parts).reshape((-1,) + (1,) * (len(shape) - axis_at - 1))

    gain = one(*shards[0])
    for cut in shards[1:]:
        gain = gain * one(*cut)
    return gain


def split_up(amount, total, limit, lean):
    weights = [(1 << 20) // math.isqrt(standing ** lean) + 1 for standing in range(2, amount + 1)]
    surplus, counts = total - limit - (amount - 1), [1] * (amount - 1)
    while surplus > 0:
        free = [i for i in range(amount - 1) if counts[i] < limit]
        whole, left = sum([weights[i] for i in free]), surplus
        for i in free:
            more = min(limit - counts[i], max(1, left * weights[i] // whole), surplus)
            counts[i] = counts[i] + more
            surplus = surplus - more
    return np.array([limit] + counts)


def uneven_parts(own_key, count, total, most, slope):
    if count == 2:
        one = jax.random.randint(own_key, (), max(1, total - most), min(most, total - 1) + 1)
        return jnp.stack([one, total - one])
    tallies = jnp.asarray(split_up(count, total, most, slope), jnp.int32)
    twos = (count - 1) // 2
    source_of, sink = tallies[1:1 + 2 * twos:2], tallies[2:2 + 2 * twos:2]
    margin = jnp.minimum(source_of - 1, most - sink)
    passed = jax.random.randint(jax.random.fold_in(own_key, 1), (twos,), 0, 1 << 20) % (margin + 1)
    tallies = tallies.at[1:1 + 2 * twos:2].set(source_of - passed).at[2:2 + 2 * twos:2].set(sink + passed)
    return tallies[jax.random.permutation(jax.random.fold_in(own_key, 2), count)]


def normal_values(stream_key, dims, scale, limit, cuts=(), kind=jnp.bfloat16):
    gain = block_levels(stream_key, dims, cuts, -0.22, 0.18) if cuts else 1.0
    array = jax.random.normal(stream_key, dims, jnp.float32) * scale * gain
    return jnp.minimum(jnp.maximum(array, -limit), limit).astype(kind)


def setup_inputs(seed: int = 0) -> dict:
    splits = jax.random.split(jax.random.key(seed), 8)
    return {
        "response_query": draw_response_query(jax.random.fold_in(splits[7], 71), 0),
        "response_kv": normal_values(splits[1], (RESP, RMAX, 2, KVH * HD), 1.0, 6.0, ((0, 128), (3, 2))),
        "prompt_cache": draw_prompt_cache(jax.random.fold_in(splits[7], 71), 0),
        "prompt_order": jax.random.permutation(splits[3], PROMPTS).astype(jnp.int32),
        "response_prompt": with_ends(jax.random.randint(splits[4], (RESP,), 0, PROMPTS), jax.random.fold_in(splits[4], 1), 0, PROMPTS - 1).astype(jnp.int32),
        "response_length": uneven_parts(splits[5], RESP, RESP * RMAX // 2, RMAX, 2).astype(jnp.int32),
        "out_grad": normal_values(splits[6], (RESP, RMAX, HQ * HD), 1.0, 6.0, ((0, 128), (2, 2))),
    }


def response_step(query, key_rows, value_rows, out_grad, length):
    total_rows = query.shape[0]
    width = key_rows.shape[0]
    scale = 1.0 / math.sqrt(HD)
    position = lax.broadcasted_iota(jnp.int32, (total_rows, width), 0)
    column = lax.broadcasted_iota(jnp.int32, (total_rows, width), 1)
    offset = column - PLEN
    allowed = (column < PLEN) | (offset <= position) & (offset < length)
    live_rows = lax.broadcasted_iota(jnp.int32, (total_rows, 1), 0) < length
    query_full = query.astype(jnp.float32)
    key_full = key_rows.astype(jnp.float32)
    value_full = value_rows.astype(jnp.float32)
    scores = jnp.einsum('tkgd,lkd->kgtl', query_full, key_full) * scale
    scores = jnp.where(allowed, scores, -1e+30)
    highest = lax.optimization_barrier(jnp.max(scores, axis=-1, keepdims=True))
    raised = jnp.exp(scores - highest)
    probs = raised / lax.optimization_barrier(jnp.sum(raised, axis=-1, keepdims=True)) * live_rows.astype(jnp.float32)
    probs_low = lax.optimization_barrier(probs.astype(jnp.bfloat16))
    probs_back = probs_low.astype(jnp.float32)
    result = jnp.einsum('kgtl,lkd->tkgd', probs_back, value_full).astype(jnp.bfloat16)
    grad_live = jnp.where(live_rows.reshape(total_rows, 1, 1, 1), out_grad, jnp.zeros_like(out_grad))
    grad_full = grad_live.astype(jnp.float32)
    dprobs = jnp.einsum('tkgd,lkd->kgtl', grad_full, value_full)
    center = lax.optimization_barrier(jnp.sum(probs * dprobs, axis=-1, keepdims=True))
    dscores = lax.optimization_barrier((probs * (dprobs - center)).astype(jnp.bfloat16))
    dscores_back = dscores.astype(jnp.float32)
    query_grad = (jnp.einsum('kgtl,lkd->tkgd', dscores_back, key_full) * scale).astype(jnp.bfloat16)
    key_grad = jnp.einsum('kgtl,tkgd->lkd', dscores_back, query_full) * scale
    value_grad = jnp.einsum('kgtl,tkgd->lkd', probs_back, grad_full)
    return (result, query_grad, key_grad, value_grad)

def reference(response_query, response_kv, prompt_cache, prompt_order, response_prompt, response_length, out_grad):
    group = HQ // KVH
    blocks = jnp.arange(PROMPTS, dtype=jnp.int32)

    def visit(carry, items):
        query, own_rows, grad, owner, length = items
        block = jnp.sum(jnp.where(prompt_order == owner, blocks, 0)).astype(jnp.int32)
        prefix = lax.dynamic_index_in_dim(prompt_cache, block, 1, keepdims=False)
        key_rows = jnp.concatenate([prefix[:, 0], own_rows[:, 0]], 0).reshape(PLEN + RMAX, KVH, HD)
        value_rows = jnp.concatenate([prefix[:, 1], own_rows[:, 1]], 0).reshape(PLEN + RMAX, KVH, HD)
        shaped = query.reshape(RMAX, KVH, group, HD)
        grad_shaped = grad.reshape(RMAX, KVH, group, HD)
        result, query_grad, key_grad, value_grad = response_step(shaped, key_rows, value_rows, grad_shaped, length)
        paired = jnp.stack([key_grad, value_grad], 1).reshape(PLEN + RMAX, 2, KVH * HD)
        current = lax.dynamic_index_in_dim(carry, block, 1, keepdims=False)
        carry = lax.dynamic_update_index_in_dim(carry, current + paired[:PLEN], block, 1)
        return (carry, (result.reshape(RMAX, HQ * HD), query_grad.reshape(RMAX, HQ * HD), paired[PLEN:].astype(jnp.bfloat16)))
    initial = jnp.zeros((PLEN, PROMPTS, 2, KVH * HD), jnp.float32)
    final, outputs = lax.scan(visit, initial, (response_query, response_kv, out_grad, response_prompt, response_length))
    attention_out, query_grad, response_kv_grad = outputs
    return (attention_out, query_grad, response_kv_grad, final.astype(jnp.bfloat16))
```

```python
import functools
import math

import jax
import jax.numpy as jnp
from jax import lax
from jax.experimental import pallas as pl
from jax.experimental.pallas import tpu as pltpu
from jax.sharding import PartitionSpec as P

HQ = 40
KVH = 8
HD = 128
PLEN = 128
RMAX = 512
GROUP = HQ // KVH
ROWS = 128
TILES = RMAX // ROWS
STACK = GROUP * ROWS
STARTS = (0, 128, 384, 768)
WIDE = 1280
SCALE = 1.0 / math.sqrt(HD)
LOG2 = SCALE * math.log2(math.e)
F32 = jnp.float32
BF16 = jnp.bfloat16
MESH = pl.DeviceIdType.MESH


def dot_nn(a, b):
    return lax.dot_general(a, b, (((1,), (0,)), ((), ())), preferred_element_type=F32)


def dot_nt(a, b):
    return lax.dot_general(a, b, (((1,), (1,)), ((), ())), preferred_element_type=F32)


def dot_tn(a, b):
    return lax.dot_general(a, b, (((0,), (0,)), ((), ())), preferred_element_type=F32)


class Grid:
    def __init__(self, seq, tp, blocks):
        self.nb = 16 if seq >= 128 else 4
        self.na = seq // self.nb
        self.nt = tp
        self.nu = self.na * tp
        self.bl = blocks // tp
        self.c1 = self.bl * 2
        self.c2 = self.na * 2

    def here(self):
        seq, t = lax.axis_index("seq"), lax.axis_index("tp")
        a, b = seq // self.nb, lax.rem(seq, self.nb)
        return a, b, t, a * self.nt + t

    def plane(self, u, b):
        return {"seq": (u // self.nt) * self.nb + b, "tp": lax.rem(u, self.nt)}

    def column(self, a, b, t):
        return {"seq": a * self.nb + b, "tp": t}


def greet(grid):
    a, b, t, u = grid.here()
    barrier = pltpu.get_barrier_semaphore()

    def plane(o, carry):
        peer = lax.rem(u + o, grid.nu)
        pl.semaphore_signal(barrier, inc=1, device_id=grid.plane(peer, b), device_id_type=MESH)
        return carry

    def column(o, carry):
        peer = lax.rem(b + o, grid.nb)
        pl.semaphore_signal(barrier, inc=1, device_id=grid.column(a, peer, t), device_id_type=MESH)
        return carry

    lax.fori_loop(1, grid.nu, plane, 0)
    lax.fori_loop(1, grid.nb, column, 0)
    pl.semaphore_wait(barrier, grid.nu + grid.nb - 2)


def plane_copy(grid, o, source, target, send, recv):
    a, b, t, u = grid.here()
    peer = lax.rem(u + o, grid.nu)
    return pltpu.make_async_remote_copy(
        src_ref=source(peer),
        dst_ref=target(u),
        send_sem=send.at[o],
        recv_sem=recv.at[o],
        device_id=grid.plane(peer, b),
        device_id_type=MESH,
    )


def column_copy(grid, o, source, target, send, recv):
    a, b, t, u = grid.here()
    peer = lax.rem(b + o, grid.nb)
    return pltpu.make_async_remote_copy(
        src_ref=source(peer),
        dst_ref=target(b),
        send_sem=send.at[o],
        recv_sem=recv.at[o],
        device_id=grid.column(a, peer, t),
        device_id_type=MESH,
    )


def start_all(copy, count):
    def step(o, carry):
        copy(o).start()
        return carry

    lax.fori_loop(1, count, step, 0)


def wait_recv_all(copy, count):
    def step(o, carry):
        copy(o).wait_recv()
        return carry

    lax.fori_loop(1, count, step, 0)


def wait_send_all(copy, count):
    def step(o, carry):
        copy(o).wait_send()
        return carry

    lax.fori_loop(1, count, step, 0)


def chunk(ref, size):
    return lambda i: ref.at[pl.ds(pl.multiple_of(i * size, size), size)]


def choice(grid, picks):
    rows, cols = grid.nb * grid.c2, grid.nu * grid.c1
    row = lax.broadcasted_iota(jnp.int32, (rows, cols), 0)
    col = lax.broadcasted_iota(jnp.int32, (rows, cols), 1)
    inner = row % grid.c2
    kv, a = inner // grid.na, inner % grid.na
    wanted = a * (grid.nt * grid.c1) + picks.astype(jnp.int32) * 2 + kv
    return jnp.where(col == wanted, 1.0, 0.0).astype(BF16)


def shuffle(grid):
    rows = grid.nb * grid.c2
    row = lax.broadcasted_iota(jnp.int32, (rows, rows), 0)
    col = lax.broadcasted_iota(jnp.int32, (rows, rows), 1)
    half = grid.nb * grid.na
    kv, b, a = row // half, (row % half) // grid.na, row % grid.na
    return jnp.where(col == b * grid.c2 + kv * grid.na + a, 1.0, 0.0).astype(BF16)


def gather_kernel(
    grid,
    cache_ref,
    order_ref,
    owner_ref,
    rows_ref,
    pick_ref,
    mark,
    marks,
    first,
    chosen,
    second,
    send_m,
    recv_m,
    send_1,
    recv_1,
    send_2,
    recv_2,
):
    a, b, t, u = grid.here()
    greet(grid)
    first_copy = lambda o: plane_copy(
        grid, o, lambda peer: cache_ref.at[lax.rem(peer, grid.nt)], chunk(first, grid.c1), send_1, recv_1
    )
    start_all(first_copy, grid.nu)
    owner = owner_ref[0]
    block = jnp.int32(0)
    for i in range(order_ref.shape[0]):
        block = block + jnp.where(order_ref[i] == owner, i, 0)
    mark[...] = jnp.full(mark.shape, block.astype(F32), F32)
    mark_copy = lambda o: column_copy(grid, o, lambda peer: mark, chunk(marks, grid.c2), send_m, recv_m)
    start_all(mark_copy, grid.nb)
    first[pl.ds(pl.multiple_of(u * grid.c1, grid.c1), grid.c1)] = cache_ref[t]
    marks[pl.ds(pl.multiple_of(b * grid.c2, grid.c2), grid.c2)] = mark[...]
    wait_recv_all(mark_copy, grid.nb)
    wide = grid.nu * grid.c1 // marks.shape[1]
    pick = choice(grid, jnp.concatenate([marks[...]] * wide, 1) if wide > 1 else marks[:, : grid.nu * grid.c1])
    pick_ref[...] = pick
    wait_recv_all(first_copy, grid.nu)
    chosen[...] = dot_nn(pick, first[...]).astype(BF16)
    second_copy = lambda o: column_copy(grid, o, chunk(chosen, grid.c2), chunk(second, grid.c2), send_2, recv_2)
    start_all(second_copy, grid.nb)
    mine = pl.ds(pl.multiple_of(b * grid.c2, grid.c2), grid.c2)
    second[mine] = chosen[mine]
    wait_recv_all(second_copy, grid.nb)
    rows_ref[...] = dot_nn(shuffle(grid), second[...]).astype(BF16)
    wait_send_all(first_copy, grid.nu)
    wait_send_all(mark_copy, grid.nb)
    wait_send_all(second_copy, grid.nb)


def reduce_kernel(
    grid,
    terms_ref,
    pick_ref,
    out_ref,
    outgoing,
    third,
    dense,
    fourth,
    send_3,
    recv_3,
    send_4,
    recv_4,
):
    a, b, t, u = grid.here()
    outgoing[...] = dot_tn(shuffle(grid), terms_ref[...]).astype(BF16)
    greet(grid)
    third_copy = lambda o: column_copy(grid, o, chunk(outgoing, grid.c2), chunk(third, grid.c2), send_3, recv_3)
    start_all(third_copy, grid.nb)
    mine = pl.ds(pl.multiple_of(b * grid.c2, grid.c2), grid.c2)
    third[mine] = outgoing[mine]
    wait_recv_all(third_copy, grid.nb)
    dense[...] = dot_tn(pick_ref[...], third[...]).astype(BF16)
    fourth_copy = lambda o: plane_copy(grid, o, chunk(dense, grid.c1), chunk(fourth, grid.c1), send_4, recv_4)
    start_all(fourth_copy, grid.nu)
    own = pl.ds(pl.multiple_of(u * grid.c1, grid.c1), grid.c1)
    fourth[own] = dense[own]
    wait_recv_all(fourth_copy, grid.nu)
    for half in range(grid.nt):
        total = jnp.zeros((grid.c1, fourth.shape[1]), F32)
        for at in range(half, grid.nu, grid.nt):
            total = total + fourth[at * grid.c1 : (at + 1) * grid.c1].astype(F32)
        out_ref[half] = total.astype(BF16)
    wait_send_all(third_copy, grid.nb)
    wait_send_all(fourth_copy, grid.nu)


def attend_kernel(
    length_ref,
    q_ref,
    g_ref,
    k_ref,
    v_ref,
    rows_ref,
    out_ref,
    dq_ref,
    dk_ref,
    dv_ref,
    terms_ref,
    scores,
    dprobs,
    raised,
    front,
    center,
    inverse,
    scaled_q,
    scaled_g,
    sum_k,
    sum_v,
):
    heads = k_ref.shape[1] // HD
    length = length_ref[0]

    def stacked(ref, kv, i):
        return jnp.concatenate(
            [
                ref[i * ROWS : (i + 1) * ROWS, pl.ds(pl.multiple_of(kv * STACK + h * HD, HD), HD)]
                for h in range(GROUP)
            ],
            0,
        )

    def lanes(kv):
        return pl.ds(pl.multiple_of(kv * HD, HD), HD)

    def own_scores(kv, carry):
        for i in range(TILES):
            seen = (i + 1) * ROWS
            scores[:, STARTS[i] : STARTS[i] + seen] = dot_nt(stacked(q_ref, kv, i), k_ref[:seen, lanes(kv)])
            dprobs[:, STARTS[i] : STARTS[i] + seen] = dot_nt(stacked(g_ref, kv, i), v_ref[:seen, lanes(kv)])
        return carry

    tri = lax.broadcasted_iota(jnp.int32, (ROWS, ROWS), 1) <= lax.broadcasted_iota(jnp.int32, (ROWS, ROWS), 0)
    rows_at = lax.broadcasted_iota(jnp.int32, (ROWS, HD), 0)

    def prompt_part(kv, carry):
        front_k = rows_ref[:PLEN, lanes(kv)]
        front_v = rows_ref[PLEN:, lanes(kv)]
        term_k = jnp.zeros((PLEN, HD), F32)
        term_v = jnp.zeros((PLEN, HD), F32)
        for i in range(TILES):
            seen = (i + 1) * ROWS
            base = STARTS[i]
            query = stacked(q_ref, kv, i)
            grad = stacked(g_ref, kv, i)
            first = dot_nt(query, front_k)
            first_dp = dot_nt(grad, front_v)
            first_e = []
            for h in range(GROUP):
                part = slice(h * ROWS, (h + 1) * ROWS)
                f = first[part]
                own = [scores[part, base + j * ROWS : base + (j + 1) * ROWS] for j in range(i + 1)]
                own[i] = jnp.where(tri, own[i], -1e30)
                top = f
                for piece in own:
                    top = jnp.maximum(top, piece)
                top = jnp.max(top, axis=-1, keepdims=True)
                first_e.append(jnp.exp2((f - top) * LOG2).astype(BF16))
                for j in range(i + 1):
                    raised[part, base + j * ROWS : base + (j + 1) * ROWS] = jnp.exp2(
                        (own[j] - top) * LOG2
                    ).astype(BF16)
            first_e = jnp.concatenate(first_e, 0)
            both = jnp.concatenate([front_v, v_ref[:seen, lanes(kv)]], 0)
            both = jnp.concatenate([both, jnp.ones((PLEN + seen, HD), BF16)], 1)
            weights = jnp.concatenate([first_e, raised[:, base : base + seen]], 1)
            result = dot_nn(weights, both)
            live = rows_at + i * ROWS < length
            first_s, new_q, new_g = [], [], []
            for h in range(GROUP):
                part = slice(h * ROWS, (h + 1) * ROWS)
                inv = jnp.where(live, 1.0 / result[part, HD:], 0.0)
                value = result[part, :HD] * inv
                out_ref[i * ROWS : (i + 1) * ROWS, pl.ds(pl.multiple_of(kv * STACK + h * HD, HD), HD)] = value.astype(
                    BF16
                )
                gf = grad[part].astype(F32)
                mid = jnp.broadcast_to(jnp.sum(gf * value, axis=-1, keepdims=True), (ROWS, HD))
                center[i, part] = mid
                inverse[i, part] = inv * SCALE
                new_q.append((query[part].astype(F32) * (inv * SCALE)).astype(BF16))
                new_g.append((gf * inv).astype(BF16))
                first_s.append((first_e[part].astype(F32) * (first_dp[part] - mid)).astype(BF16))
            first_s = jnp.concatenate(first_s, 0)
            new_q = jnp.concatenate(new_q, 0)
            new_g = jnp.concatenate(new_g, 0)
            front[i] = first_s
            scaled_q[i] = new_q
            scaled_g[i] = new_g
            term_k = term_k + dot_tn(first_s, new_q)
            term_v = term_v + dot_tn(first_e, new_g)
        terms_ref[:PLEN, lanes(kv)] = term_k.astype(BF16)
        terms_ref[PLEN:, lanes(kv)] = term_v.astype(BF16)
        return carry

    def own_part(kv, carry):
        front_k = rows_ref[:PLEN, lanes(kv)]
        sum_k[...] = jnp.zeros_like(sum_k)
        sum_v[...] = jnp.zeros_like(sum_v)
        for i in range(TILES):
            seen = (i + 1) * ROWS
            base = STARTS[i]
            weights = raised[:, base : base + seen]
            own_s = []
            for j in range(i + 1):
                at = base + j * ROWS
                own_s.append(
                    jnp.concatenate(
                        [
                            (
                                raised[h * ROWS : (h + 1) * ROWS, at : at + ROWS].astype(F32)
                                * (
                                    dprobs[h * ROWS : (h + 1) * ROWS, at : at + ROWS]
                                    - center[i, h * ROWS : (h + 1) * ROWS]
                                )
                            ).astype(BF16)
                            for h in range(GROUP)
                        ],
                        0,
                    )
                )
            own_s = jnp.concatenate(own_s, 1)
            keys = jnp.concatenate([front_k, k_ref[:seen, lanes(kv)]], 0)
            grad_q = dot_nn(jnp.concatenate([front[i], own_s], 1), keys) * inverse[i]
            for h in range(GROUP):
                dq_ref[i * ROWS : (i + 1) * ROWS, pl.ds(pl.multiple_of(kv * STACK + h * HD, HD), HD)] = grad_q[
                    h * ROWS : (h + 1) * ROWS
                ].astype(BF16)
            sum_k[:seen] += dot_tn(own_s, scaled_q[i])
            sum_v[:seen] += dot_tn(weights, scaled_g[i])
        dk_ref[:, lanes(kv)] = sum_k[...].astype(BF16)
        dv_ref[:, lanes(kv)] = sum_v[...].astype(BF16)
        return carry

    def head(kv, carry):
        own_scores(kv, carry)
        prompt_part(kv, carry)
        own_part(kv, carry)
        return carry

    lax.fori_loop(0, heads, head, 0)


def attend(length, q, g, k, v, rows):
    heads = k.shape[1] // HD
    vmem = pl.BlockSpec(memory_space=pltpu.VMEM)
    stack = (TILES, STACK, HD)
    return pl.pallas_call(
        attend_kernel,
        out_shape=(
            jax.ShapeDtypeStruct(q.shape, BF16),
            jax.ShapeDtypeStruct(q.shape, BF16),
            jax.ShapeDtypeStruct(k.shape, BF16),
            jax.ShapeDtypeStruct(k.shape, BF16),
            jax.ShapeDtypeStruct(rows.shape, BF16),
        ),
        in_specs=[pl.BlockSpec(memory_space=pltpu.SMEM)] + [vmem] * 5,
        out_specs=(vmem,) * 5,
        scratch_shapes=[
            pltpu.VMEM((STACK, WIDE), F32),
            pltpu.VMEM((STACK, WIDE), F32),
            pltpu.VMEM((STACK, WIDE), BF16),
            pltpu.VMEM(stack, BF16),
            pltpu.VMEM(stack, F32),
            pltpu.VMEM(stack, F32),
            pltpu.VMEM(stack, BF16),
            pltpu.VMEM(stack, BF16),
            pltpu.VMEM((RMAX, HD), F32),
            pltpu.VMEM((RMAX, HD), F32),
        ],
        compiler_params=pltpu.CompilerParams(vmem_limit_bytes=63 * 1024 * 1024),
    )(length, q, g, k, v, rows)


def local(
    grid,
    response_query,
    response_kv,
    prompt_cache,
    prompt_order,
    response_prompt,
    response_length,
    out_grad,
):
    width = response_kv.shape[3]
    vmem = pl.BlockSpec(memory_space=pltpu.VMEM)
    smem = pl.BlockSpec(memory_space=pltpu.SMEM)
    dma = pltpu.SemaphoreType.DMA
    cache = prompt_cache.reshape(grid.c1, grid.nt, width).transpose(1, 0, 2)
    all_rows = grid.nb * grid.c2
    all_blocks = grid.nu * grid.c1
    rows, pick = pl.pallas_call(
        functools.partial(gather_kernel, grid),
        out_shape=(
            jax.ShapeDtypeStruct((all_rows, width), BF16),
            jax.ShapeDtypeStruct((all_rows, all_blocks), BF16),
        ),
        in_specs=[vmem, smem, smem],
        out_specs=(vmem, vmem),
        scratch_shapes=[
            pltpu.VMEM((grid.c2, HD), F32),
            pltpu.VMEM((all_rows, HD), F32),
            pltpu.VMEM((all_blocks, width), BF16),
            pltpu.VMEM((all_rows, width), BF16),
            pltpu.VMEM((all_rows, width), BF16),
            dma((grid.nb,)),
            dma((grid.nb,)),
            dma((grid.nu,)),
            dma((grid.nu,)),
            dma((grid.nb,)),
            dma((grid.nb,)),
        ],
        compiler_params=pltpu.CompilerParams(collective_id=0, has_side_effects=True),
    )(cache, prompt_order, response_prompt)
    out, dq, dk, dv, terms = attend(
        response_length, response_query[0], out_grad[0], response_kv[0, :, 0], response_kv[0, :, 1], rows
    )
    summed = pl.pallas_call(
        functools.partial(reduce_kernel, grid),
        out_shape=jax.ShapeDtypeStruct((grid.nt, grid.c1, width), BF16),
        in_specs=[vmem, vmem],
        out_specs=vmem,
        scratch_shapes=[
            pltpu.VMEM((all_rows, width), BF16),
            pltpu.VMEM((all_rows, width), BF16),
            pltpu.VMEM((all_blocks, width), BF16),
            pltpu.VMEM((all_blocks, width), BF16),
            dma((grid.nb,)),
            dma((grid.nb,)),
            dma((grid.nu,)),
            dma((grid.nu,)),
        ],
        compiler_params=pltpu.CompilerParams(collective_id=1, has_side_effects=True),
    )(terms, pick)
    prompt_cache_grad = summed.transpose(1, 0, 2).reshape(prompt_cache.shape)
    return (out[None], dq[None], jnp.stack([dk, dv], 1)[None], prompt_cache_grad)


def solution(mesh):
    grid = Grid(mesh.shape["seq"], mesh.shape["tp"], 16)
    return jax.shard_map(
        functools.partial(local, grid),
        mesh=mesh,
        in_specs=(
            P("seq", None, "tp"),
            P("seq", None, None, "tp"),
            P("seq", "tp", None, None),
            P(),
            P("seq"),
            P("seq"),
            P("seq", None, "tp"),
        ),
        out_specs=(
            P("seq", None, "tp"),
            P("seq", None, "tp"),
            P("seq", None, None, "tp"),
            P("seq", "tp", None, None),
        ),
        check_vma=False,
    )
```

```python
import functools
import math

import jax
import jax.numpy as jnp
from jax import lax
from jax.experimental import pallas as pl
from jax.experimental.pallas import tpu as pltpu
from jax.sharding import PartitionSpec as P

HQ = 40
KVH = 8
HD = 128
PLEN = 128
RMAX = 512
GROUP = HQ // KVH
ROWS = 128
TILES = RMAX // ROWS
STACK = GROUP * ROWS
STARTS = (0, 128, 384, 768)
WIDE = 1280
SCALE = 1.0 / math.sqrt(HD)
LOG2 = SCALE * math.log2(math.e)
F32 = jnp.float32
BF16 = jnp.bfloat16
MESH = pl.DeviceIdType.MESH


def dot_nn(a, b):
    return lax.dot_general(a, b, (((1,), (0,)), ((), ())), preferred_element_type=F32)


def dot_nt(a, b):
    return lax.dot_general(a, b, (((1,), (1,)), ((), ())), preferred_element_type=F32)


def dot_tn(a, b):
    return lax.dot_general(a, b, (((0,), (0,)), ((), ())), preferred_element_type=F32)


class Grid:
    def __init__(self, seq, tp, blocks):
        self.nb = 16 if seq >= 128 else 4
        self.na = seq // self.nb
        self.nt = tp
        self.nu = self.na * tp
        self.bl = blocks // tp
        self.c1 = self.bl * 2
        self.c2 = self.na * 2

    def here(self):
        seq, t = lax.axis_index("seq"), lax.axis_index("tp")
        a, b = seq // self.nb, lax.rem(seq, self.nb)
        return a, b, t, a * self.nt + t

    def plane(self, u, b):
        return {"seq": (u // self.nt) * self.nb + b, "tp": lax.rem(u, self.nt)}

    def column(self, a, b, t):
        return {"seq": a * self.nb + b, "tp": t}


def greet(grid):
    a, b, t, u = grid.here()
    barrier = pltpu.get_barrier_semaphore()

    def plane(o, carry):
        peer = lax.rem(u + o, grid.nu)
        pl.semaphore_signal(barrier, inc=1, device_id=grid.plane(peer, b), device_id_type=MESH)
        return carry

    def column(o, carry):
        peer = lax.rem(b + o, grid.nb)
        pl.semaphore_signal(barrier, inc=1, device_id=grid.column(a, peer, t), device_id_type=MESH)
        return carry

    lax.fori_loop(1, grid.nu, plane, 0)
    lax.fori_loop(1, grid.nb, column, 0)
    pl.semaphore_wait(barrier, grid.nu + grid.nb - 2)


def plane_copy(grid, o, source, target, send, recv):
    a, b, t, u = grid.here()
    peer = lax.rem(u + o, grid.nu)
    return pltpu.make_async_remote_copy(
        src_ref=source(peer),
        dst_ref=target(u),
        send_sem=send.at[o],
        recv_sem=recv.at[o],
        device_id=grid.plane(peer, b),
        device_id_type=MESH,
    )


def column_copy(grid, o, source, target, send, recv):
    a, b, t, u = grid.here()
    peer = lax.rem(b + o, grid.nb)
    return pltpu.make_async_remote_copy(
        src_ref=source(peer),
        dst_ref=target(b),
        send_sem=send.at[o],
        recv_sem=recv.at[o],
        device_id=grid.column(a, peer, t),
        device_id_type=MESH,
    )


def start_all(copy, count):
    def step(o, carry):
        copy(o).start()
        return carry

    lax.fori_loop(1, count, step, 0)


def wait_recv_all(copy, count):
    def step(o, carry):
        copy(o).wait_recv()
        return carry

    lax.fori_loop(1, count, step, 0)


def wait_send_all(copy, count):
    def step(o, carry):
        copy(o).wait_send()
        return carry

    lax.fori_loop(1, count, step, 0)


def chunk(ref, size):
    return lambda i: ref.at[pl.ds(pl.multiple_of(i * size, size), size)]


def choice(grid, picks):
    rows, cols = grid.nb * grid.c2, grid.nu * grid.c1
    row = lax.broadcasted_iota(jnp.int32, (rows, cols), 0)
    col = lax.broadcasted_iota(jnp.int32, (rows, cols), 1)
    inner = row % grid.c2
    kv, a = inner // grid.na, inner % grid.na
    wanted = a * (grid.nt * grid.c1) + picks.astype(jnp.int32) * 2 + kv
    return jnp.where(col == wanted, 1.0, 0.0).astype(BF16)


def shuffle(grid):
    rows = grid.nb * grid.c2
    row = lax.broadcasted_iota(jnp.int32, (rows, rows), 0)
    col = lax.broadcasted_iota(jnp.int32, (rows, rows), 1)
    half = grid.nb * grid.na
    kv, b, a = row // half, (row % half) // grid.na, row % grid.na
    return jnp.where(col == b * grid.c2 + kv * grid.na + a, 1.0, 0.0).astype(BF16)


def pairs():
    row = lax.broadcasted_iota(jnp.int32, (2 * ROWS, 2 * ROWS), 0)
    col = lax.broadcasted_iota(jnp.int32, (2 * ROWS, 2 * ROWS), 1)
    return jnp.where(col == (row % ROWS) * 2 + row // ROWS, 1.0, 0.0).astype(BF16)


def kernel(
    grid,
    order_ref,
    owner_ref,
    length_ref,
    cache_ref,
    kv_ref,
    q_hbm,
    g_hbm,
    out_hbm,
    dq_hbm,
    dkv_ref,
    cgrad_ref,
    mark,
    marks,
    first,
    pick,
    chosen,
    second,
    rows,
    terms,
    outgoing,
    third,
    dense,
    fourth,
    q_buf,
    g_buf,
    out_buf,
    dq_buf,
    k_own,
    v_own,
    scores,
    raised,
    memo_o,
    memo_l,
    memo_m,
    front,
    sum_k,
    sum_v,
    in_sem,
    out_sem,
    send_m,
    recv_m,
    send_1,
    recv_1,
    send_2,
    recv_2,
    send_3,
    recv_3,
    send_4,
    recv_4,
):
    a, b, t, u = grid.here()
    heads = q_buf.shape[0]
    width = k_own.shape[1]
    half = width // 2
    length = length_ref[0]

    def moved(kv):
        return pl.ds(pl.multiple_of(kv * STACK, STACK), STACK)

    def load_q(kv):
        return pltpu.make_async_copy(q_hbm.at[:, moved(kv)], q_buf.at[kv], in_sem.at[0, kv])

    def load_g(kv):
        return pltpu.make_async_copy(g_hbm.at[:, moved(kv)], g_buf.at[kv], in_sem.at[1, kv])

    def save_out(kv):
        return pltpu.make_async_copy(out_buf.at[kv], out_hbm.at[:, moved(kv)], out_sem.at[0, kv])

    def save_dq(kv):
        return pltpu.make_async_copy(dq_buf.at[kv], dq_hbm.at[:, moved(kv)], out_sem.at[1, kv])

    def stacked(ref, kv, i):
        return jnp.concatenate(
            [ref[kv, i * ROWS : (i + 1) * ROWS, h * HD : (h + 1) * HD] for h in range(GROUP)], 0
        )

    def lanes(kv):
        return pl.ds(pl.multiple_of(kv * HD, HD), HD)

    tri = lax.broadcasted_iota(jnp.int32, (ROWS, ROWS), 1) <= lax.broadcasted_iota(jnp.int32, (ROWS, ROWS), 0)
    rows_at = lax.broadcasted_iota(jnp.int32, (ROWS, HD), 0)

    def own_forward(kv, carry):
        load_q(kv).wait()
        for i in range(TILES):
            seen = (i + 1) * ROWS
            base = STARTS[i]
            scores[:, base : base + seen] = dot_nt(stacked(q_buf, kv, i), k_own[:seen, lanes(kv)])
            for h in range(GROUP):
                part = slice(h * ROWS, (h + 1) * ROWS)
                own = [scores[part, base + j * ROWS : base + (j + 1) * ROWS] for j in range(i + 1)]
                own[i] = jnp.where(tri, own[i], -1e30)
                top = own[0]
                for piece in own[1:]:
                    top = jnp.maximum(top, piece)
                top = jnp.max(top, axis=-1, keepdims=True)
                memo_m[kv, i, part] = jnp.broadcast_to(top, (ROWS, HD))
                for j in range(i + 1):
                    raised[kv, part, base + j * ROWS : base + (j + 1) * ROWS] = jnp.exp2(
                        (own[j] - top) * LOG2
                    ).astype(BF16)
            both = jnp.concatenate([v_own[:seen, lanes(kv)], jnp.ones((seen, HD), BF16)], 1)
            result = dot_nn(raised[kv, :, base : base + seen], both)
            memo_o[kv, i] = result[:, :HD]
            memo_l[kv, i] = result[:, HD:]
        return carry

    def prompt_part(kv, carry):
        load_g(kv).wait()
        front_k = rows[:PLEN, lanes(kv)]
        front_v = rows[PLEN:, lanes(kv)]
        both = jnp.concatenate([front_v, jnp.ones((PLEN, HD), BF16)], 1)
        term_k = jnp.zeros((PLEN, HD), F32)
        term_v = jnp.zeros((PLEN, HD), F32)
        for i in range(TILES):
            query = stacked(q_buf, kv, i)
            grad = stacked(g_buf, kv, i)
            first_s = dot_nt(query, front_k)
            first_dp = dot_nt(grad, front_v)
            first_e, alphas = [], []
            for h in range(GROUP):
                part = slice(h * ROWS, (h + 1) * ROWS)
                own_top = memo_m[kv, i, part]
                top = jnp.maximum(jnp.max(first_s[part], axis=-1, keepdims=True), own_top)
                first_e.append(jnp.exp2((first_s[part] - top) * LOG2).astype(BF16))
                alphas.append(jnp.exp2((own_top - top) * LOG2))
            first_e = jnp.concatenate(first_e, 0)
            result = dot_nn(first_e, both)
            live = rows_at + i * ROWS < length
            first_d, new_q, new_g = [], [], []
            for h in range(GROUP):
                part = slice(h * ROWS, (h + 1) * ROWS)
                alpha = alphas[h]
                total = alpha * memo_l[kv, i, part] + result[part, HD:]
                inv = jnp.where(live, 1.0 / total, 0.0)
                value = (alpha * memo_o[kv, i, part] + result[part, :HD]) * inv
                out_buf[kv, i * ROWS : (i + 1) * ROWS, h * HD : (h + 1) * HD] = value.astype(BF16)
                gf = grad[part].astype(F32)
                mid = jnp.broadcast_to(jnp.sum(gf * value, axis=-1, keepdims=True), (ROWS, HD))
                memo_l[kv, i, part] = mid
                memo_o[kv, i, part] = inv
                memo_m[kv, i, part] = alpha * inv
                new_q.append((query[part].astype(F32) * (inv * SCALE)).astype(BF16))
                new_g.append((gf * inv).astype(BF16))
                first_d.append((first_e[part].astype(F32) * (first_dp[part] - mid)).astype(BF16))
            first_d = jnp.concatenate(first_d, 0)
            front[kv, i] = first_d
            term_k = term_k + dot_tn(first_d, jnp.concatenate(new_q, 0))
            term_v = term_v + dot_tn(first_e, jnp.concatenate(new_g, 0))
        terms[:PLEN, lanes(kv)] = term_k.astype(BF16)
        terms[PLEN:, lanes(kv)] = term_v.astype(BF16)
        save_out(kv).start()
        return carry

    def own_backward(kv, carry):
        front_k = rows[:PLEN, lanes(kv)]
        sum_k[...] = jnp.zeros_like(sum_k)
        sum_v[...] = jnp.zeros_like(sum_v)
        for i in range(TILES):
            seen = (i + 1) * ROWS
            base = STARTS[i]
            scores[:, base : base + seen] = dot_nt(stacked(g_buf, kv, i), v_own[:seen, lanes(kv)])
            own_d = jnp.concatenate(
                [
                    jnp.concatenate(
                        [
                            (
                                raised[kv, h * ROWS : (h + 1) * ROWS, base + j * ROWS : base + (j + 1) * ROWS].astype(
                                    F32
                                )
                                * (
                                    scores[h * ROWS : (h + 1) * ROWS, base + j * ROWS : base + (j + 1) * ROWS]
                                    - memo_l[kv, i, h * ROWS : (h + 1) * ROWS]
                                )
                            ).astype(BF16)
                            for h in range(GROUP)
                        ],
                        0,
                    )
                    for j in range(i + 1)
                ],
                1,
            )
            factor = memo_m[kv, i]
            new_q = (stacked(q_buf, kv, i).astype(F32) * (factor * SCALE)).astype(BF16)
            new_g = (stacked(g_buf, kv, i).astype(F32) * factor).astype(BF16)
            grad_q = dot_nn(front[kv, i], front_k) * (memo_o[kv, i] * SCALE)
            grad_q = grad_q + dot_nn(own_d, k_own[:seen, lanes(kv)]) * (factor * SCALE)
            for h in range(GROUP):
                dq_buf[kv, i * ROWS : (i + 1) * ROWS, h * HD : (h + 1) * HD] = grad_q[
                    h * ROWS : (h + 1) * ROWS
                ].astype(BF16)
            sum_k[:seen] += dot_tn(own_d, new_q)
            sum_v[:seen] += dot_tn(raised[kv, :, base : base + seen], new_g)
        order = pairs()
        for j in range(TILES):
            at = slice(j * ROWS, (j + 1) * ROWS)
            dkv_ref[2 * j * ROWS : 2 * (j + 1) * ROWS, lanes(kv)] = dot_tn(
                order, jnp.concatenate([sum_k[at].astype(BF16), sum_v[at].astype(BF16)], 0)
            ).astype(BF16)
        save_dq(kv).start()
        return carry

    def run(step, low, high):
        lax.fori_loop(low, high, step, 0)

    def first_copy(o):
        return plane_copy(
            grid,
            o,
            lambda peer: cache_ref.at[
                :, pl.ds(pl.multiple_of(lax.rem(peer, grid.nt) * width, width), width)
            ],
            chunk(first, grid.c1),
            send_1,
            recv_1,
        )

    def mark_copy(o):
        return column_copy(grid, o, lambda peer: mark, chunk(marks, grid.c2), send_m, recv_m)

    def second_copy(o):
        return column_copy(grid, o, chunk(chosen, grid.c2), chunk(second, grid.c2), send_2, recv_2)

    def third_copy(part):
        return lambda o: column_copy(
            grid,
            o,
            chunk(outgoing.at[part], grid.c2),
            chunk(third.at[part], grid.c2),
            send_3.at[part],
            recv_3.at[part],
        )

    def fourth_copy(part):
        return lambda o: plane_copy(
            grid,
            o,
            chunk(dense.at[part], grid.c1),
            chunk(fourth.at[part], grid.c1),
            send_4.at[part],
            recv_4.at[part],
        )

    in_plane = pl.ds(pl.multiple_of(u * grid.c1, grid.c1), grid.c1)
    in_column = pl.ds(pl.multiple_of(b * grid.c2, grid.c2), grid.c2)

    def send_terms(part):
        outgoing[part] = dot_tn(shuffle(grid), terms[:, part * half : (part + 1) * half]).astype(BF16)
        start_all(third_copy(part), grid.nb)
        third[part, in_column] = outgoing[part, in_column]

    def send_sums(part):
        wait_recv_all(third_copy(part), grid.nb)
        dense[part] = dot_tn(pick[...], third[part]).astype(BF16)
        start_all(fourth_copy(part), grid.nu)
        fourth[part, in_plane] = dense[part, in_plane]

    def finish(part):
        wait_recv_all(fourth_copy(part), grid.nu)
        for at_t in range(grid.nt):
            total = jnp.zeros((grid.c1, half), F32)
            for at in range(at_t, grid.nu, grid.nt):
                total = total + fourth[part, at * grid.c1 : (at + 1) * grid.c1].astype(F32)
            cgrad_ref[:, at_t * width + part * half : at_t * width + (part + 1) * half] = total.astype(BF16)

    def load_all(kv, carry):
        load_q(kv).start()
        load_g(kv).start()
        return carry

    run(load_all, 0, heads)
    block = jnp.int32(0)
    for i in range(order_ref.shape[0]):
        block = block + jnp.where(order_ref[i] == owner_ref[0], i, 0)
    mark[...] = jnp.full(mark.shape, block.astype(F32), F32)
    greet(grid)
    start_all(first_copy, grid.nu)
    start_all(mark_copy, grid.nb)
    first[in_plane] = cache_ref[:, pl.ds(pl.multiple_of(t * width, width), width)]
    marks[in_column] = mark[...]
    order = pairs()
    for j in range(TILES):
        split = dot_nn(order, kv_ref[2 * j * ROWS : 2 * (j + 1) * ROWS]).astype(BF16)
        k_own[j * ROWS : (j + 1) * ROWS] = split[:ROWS]
        v_own[j * ROWS : (j + 1) * ROWS] = split[ROWS:]
    run(own_forward, 0, 2)
    wait_recv_all(mark_copy, grid.nb)
    many = grid.nu * grid.c1 // marks.shape[1]
    pick[...] = choice(
        grid, jnp.concatenate([marks[...]] * many, 1) if many > 1 else marks[:, : grid.nu * grid.c1]
    )
    wait_recv_all(first_copy, grid.nu)
    chosen[...] = dot_nn(pick[...], first[...]).astype(BF16)
    start_all(second_copy, grid.nb)
    second[in_column] = chosen[in_column]
    run(own_forward, 2, heads)
    wait_recv_all(second_copy, grid.nb)
    rows[...] = dot_nn(shuffle(grid), second[...]).astype(BF16)
    run(prompt_part, 0, heads // 2)
    send_terms(0)
    run(prompt_part, heads // 2, heads)
    send_terms(1)
    run(own_backward, 0, 1)
    send_sums(0)
    run(own_backward, 1, 2)
    send_sums(1)
    run(own_backward, 2, heads)
    finish(0)
    finish(1)

    wait_send_all(first_copy, grid.nu)
    wait_send_all(mark_copy, grid.nb)
    wait_send_all(second_copy, grid.nb)
    for part in range(2):
        wait_send_all(third_copy(part), grid.nb)
        wait_send_all(fourth_copy(part), grid.nu)

    def saved(kv, carry):
        save_out(kv).wait()
        save_dq(kv).wait()
        return carry

    run(saved, 0, heads)


def local(
    grid,
    response_query,
    response_kv,
    prompt_cache,
    prompt_order,
    response_prompt,
    response_length,
    out_grad,
):
    width = response_kv.shape[3]
    heads = width // HD
    half = width // 2
    vmem = pl.BlockSpec(memory_space=pltpu.VMEM)
    smem = pl.BlockSpec(memory_space=pltpu.SMEM)
    hbm = pl.BlockSpec(memory_space=pl.ANY)
    dma = pltpu.SemaphoreType.DMA
    all_rows = grid.nb * grid.c2
    all_blocks = grid.nu * grid.c1
    stack = (heads, TILES, STACK, HD)
    full = (heads, RMAX, STACK)
    flat = response_query.shape[1:]
    out, dq, dkv, summed = pl.pallas_call(
        functools.partial(kernel, grid),
        out_shape=(
            jax.ShapeDtypeStruct(flat, BF16),
            jax.ShapeDtypeStruct(flat, BF16),
            jax.ShapeDtypeStruct((2 * RMAX, width), BF16),
            jax.ShapeDtypeStruct((grid.c1, grid.nt * width), BF16),
        ),
        in_specs=[smem] * 3 + [vmem] * 2 + [hbm] * 2,
        out_specs=(hbm, hbm, vmem, vmem),
        scratch_shapes=[
            pltpu.VMEM((grid.c2, HD), F32),
            pltpu.VMEM((all_rows, HD), F32),
            pltpu.VMEM((all_blocks, width), BF16),
            pltpu.VMEM((all_rows, all_blocks), BF16),
            pltpu.VMEM((all_rows, width), BF16),
            pltpu.VMEM((all_rows, width), BF16),
            pltpu.VMEM((all_rows, width), BF16),
            pltpu.VMEM((all_rows, width), BF16),
            pltpu.VMEM((2, all_rows, half), BF16),
            pltpu.VMEM((2, all_rows, half), BF16),
            pltpu.VMEM((2, all_blocks, half), BF16),
            pltpu.VMEM((2, all_blocks, half), BF16),
            pltpu.VMEM(full, BF16),
            pltpu.VMEM(full, BF16),
            pltpu.VMEM(full, BF16),
            pltpu.VMEM(full, BF16),
            pltpu.VMEM((RMAX, width), BF16),
            pltpu.VMEM((RMAX, width), BF16),
            pltpu.VMEM((STACK, WIDE), F32),
            pltpu.VMEM((heads, STACK, WIDE), BF16),
            pltpu.VMEM(stack, F32),
            pltpu.VMEM(stack, F32),
            pltpu.VMEM(stack, F32),
            pltpu.VMEM(stack, BF16),
            pltpu.VMEM((RMAX, HD), F32),
            pltpu.VMEM((RMAX, HD), F32),
            dma((2, heads)),
            dma((2, heads)),
            dma((grid.nb,)),
            dma((grid.nb,)),
            dma((grid.nu,)),
            dma((grid.nu,)),
            dma((grid.nb,)),
            dma((grid.nb,)),
            dma((2, grid.nb)),
            dma((2, grid.nb)),
            dma((2, grid.nu)),
            dma((2, grid.nu)),
        ],
        compiler_params=pltpu.CompilerParams(
            collective_id=0, has_side_effects=True, vmem_limit_bytes=62 * 1024 * 1024
        ),
    )(
        prompt_order,
        response_prompt,
        response_length,
        prompt_cache.reshape(grid.c1, grid.nt * width),
        response_kv.reshape(2 * RMAX, width),
        response_query[0],
        out_grad[0],
    )
    return (out[None], dq[None], dkv.reshape(response_kv.shape), summed.reshape(prompt_cache.shape))


def solution(mesh):
    grid = Grid(mesh.shape["seq"], mesh.shape["tp"], 16)
    return jax.shard_map(
        functools.partial(local, grid),
        mesh=mesh,
        in_specs=(
            P("seq", None, "tp"),
            P("seq", None, None, "tp"),
            P("seq", "tp", None, None),
            P(),
            P("seq"),
            P("seq"),
            P("seq", None, "tp"),
        ),
        out_specs=(
            P("seq", None, "tp"),
            P("seq", None, "tp"),
            P("seq", None, None, "tp"),
            P("seq", "tp", None, None),
        ),
        check_vma=False,
    )
```

```python
import functools
import math

import jax
import jax.numpy as jnp
from jax import lax
from jax.experimental import pallas as pl
from jax.experimental.pallas import tpu as pltpu
from jax.sharding import PartitionSpec as P

HQ = 40
KVH = 8
HD = 128
PLEN = 128
RMAX = 512
GROUP = HQ // KVH
ROWS = 128
TILES = RMAX // ROWS
STACK = GROUP * ROWS
STARTS = (0, 128, 384, 768)
WIDE = 1280
SCALE = 1.0 / math.sqrt(HD)
LOG2 = SCALE * math.log2(math.e)
F32 = jnp.float32
BF16 = jnp.bfloat16
MESH = pl.DeviceIdType.MESH


def dot_nn(a, b):
    return lax.dot_general(a, b, (((1,), (0,)), ((), ())), preferred_element_type=F32)


def dot_nt(a, b):
    return lax.dot_general(a, b, (((1,), (1,)), ((), ())), preferred_element_type=F32)


def dot_tn(a, b):
    return lax.dot_general(a, b, (((0,), (0,)), ((), ())), preferred_element_type=F32)


class Grid:
    def __init__(self, seq, tp, blocks):
        self.nb = 16 if seq >= 128 else 4
        self.na = seq // self.nb
        self.nt = tp
        self.nu = self.na * tp
        self.bl = blocks // tp
        self.c1 = self.bl * 2
        self.c2 = self.na * 2

    def here(self):
        seq, t = lax.axis_index("seq"), lax.axis_index("tp")
        a, b = seq // self.nb, lax.rem(seq, self.nb)
        return a, b, t, a * self.nt + t

    def plane(self, u, b):
        return {"seq": (u // self.nt) * self.nb + b, "tp": lax.rem(u, self.nt)}

    def column(self, a, b, t):
        return {"seq": a * self.nb + b, "tp": t}


def greet(grid):
    a, b, t, u = grid.here()
    barrier = pltpu.get_barrier_semaphore()

    def plane(o, carry):
        peer = lax.rem(u + o, grid.nu)
        pl.semaphore_signal(barrier, inc=1, device_id=grid.plane(peer, b), device_id_type=MESH)
        return carry

    def column(o, carry):
        peer = lax.rem(b + o, grid.nb)
        pl.semaphore_signal(barrier, inc=1, device_id=grid.column(a, peer, t), device_id_type=MESH)
        return carry

    lax.fori_loop(1, grid.nu, plane, 0)
    lax.fori_loop(1, grid.nb, column, 0)
    pl.semaphore_wait(barrier, grid.nu + grid.nb - 2)


def plane_copy(grid, o, source, target, send, recv):
    a, b, t, u = grid.here()
    peer = lax.rem(u + o, grid.nu)
    return pltpu.make_async_remote_copy(
        src_ref=source(peer),
        dst_ref=target(u),
        send_sem=send.at[o],
        recv_sem=recv.at[o],
        device_id=grid.plane(peer, b),
        device_id_type=MESH,
    )


def column_copy(grid, o, source, target, send, recv):
    a, b, t, u = grid.here()
    peer = lax.rem(b + o, grid.nb)
    return pltpu.make_async_remote_copy(
        src_ref=source(peer),
        dst_ref=target(b),
        send_sem=send.at[o],
        recv_sem=recv.at[o],
        device_id=grid.column(a, peer, t),
        device_id_type=MESH,
    )


def start_all(copy, count):
    def step(o, carry):
        copy(o).start()
        return carry

    lax.fori_loop(1, count, step, 0)


def wait_recv_all(copy, count):
    def step(o, carry):
        copy(o).wait_recv()
        return carry

    lax.fori_loop(1, count, step, 0)


def wait_send_all(copy, count):
    def step(o, carry):
        copy(o).wait_send()
        return carry

    lax.fori_loop(1, count, step, 0)


def chunk(ref, size):
    return lambda i: ref.at[pl.ds(pl.multiple_of(i * size, size), size)]


def choice(grid, picks):
    rows, cols = grid.nb * grid.c2, grid.nu * grid.c1
    row = lax.broadcasted_iota(jnp.int32, (rows, cols), 0)
    col = lax.broadcasted_iota(jnp.int32, (rows, cols), 1)
    inner = row % grid.c2
    kv, a = inner // grid.na, inner % grid.na
    wanted = a * (grid.nt * grid.c1) + picks.astype(jnp.int32) * 2 + kv
    return jnp.where(col == wanted, 1.0, 0.0).astype(BF16)


def shuffle(grid):
    rows = grid.nb * grid.c2
    row = lax.broadcasted_iota(jnp.int32, (rows, rows), 0)
    col = lax.broadcasted_iota(jnp.int32, (rows, rows), 1)
    half = grid.nb * grid.na
    kv, b, a = row // half, (row % half) // grid.na, row % grid.na
    return jnp.where(col == b * grid.c2 + kv * grid.na + a, 1.0, 0.0).astype(BF16)


def pairs():
    row = lax.broadcasted_iota(jnp.int32, (2 * ROWS, 2 * ROWS), 0)
    col = lax.broadcasted_iota(jnp.int32, (2 * ROWS, 2 * ROWS), 1)
    return jnp.where(col == (row % ROWS) * 2 + row // ROWS, 1.0, 0.0).astype(BF16)


def kernel(
    grid,
    order_ref,
    owner_ref,
    length_ref,
    cache_ref,
    kv_ref,
    q_hbm,
    g_hbm,
    out_ref,
    dq_ref,
    dkv_ref,
    cgrad_ref,
    cache,
    mark,
    marks,
    first,
    pick,
    chosen,
    second,
    rows,
    terms,
    outgoing,
    third,
    dense,
    fourth,
    q_buf,
    g_buf,
    k_own,
    v_own,
    raised,
    dprobs,
    stats,
    front_p,
    front_d,
    low_p,
    low_d,
    sum_k,
    sum_v,
    in_sem,
    send_m,
    recv_m,
    send_1,
    recv_1,
    send_2,
    recv_2,
    send_3,
    recv_3,
    send_4,
    recv_4,
):
    a, b, t, u = grid.here()
    heads = q_buf.shape[0]
    width = k_own.shape[1]
    half = width // 2
    length = length_ref[0]

    def moved(kv):
        return pl.ds(pl.multiple_of(kv * STACK, STACK), STACK)

    def load_q(kv):
        return pltpu.make_async_copy(q_hbm.at[:, moved(kv)], q_buf.at[kv], in_sem.at[0, kv])

    def load_g(kv):
        return pltpu.make_async_copy(g_hbm.at[:, moved(kv)], g_buf.at[kv], in_sem.at[1, kv])

    def stacked(ref, kv, i):
        return jnp.concatenate(
            [ref[kv, i * ROWS : (i + 1) * ROWS, h * HD : (h + 1) * HD] for h in range(GROUP)], 0
        )

    def lanes(kv):
        return pl.ds(pl.multiple_of(kv * HD, HD), HD)

    def head_lanes(kv, h):
        return pl.ds(pl.multiple_of(kv * STACK + h * HD, HD), HD)

    tri = lax.broadcasted_iota(jnp.int32, (ROWS, ROWS), 0) <= lax.broadcasted_iota(jnp.int32, (ROWS, ROWS), 1)
    row_at = lax.broadcasted_iota(jnp.int32, (1, ROWS), 1)

    def own_forward(kv, carry):
        load_q(kv).wait()
        load_g(kv).wait()
        for i in range(TILES):
            seen = (i + 1) * ROWS
            base = STARTS[i]
            raised[kv, base : base + seen] = dot_nt(k_own[:seen, lanes(kv)], stacked(q_buf, kv, i))
            dprobs[kv, base : base + seen] = dot_nt(v_own[:seen, lanes(kv)], stacked(g_buf, kv, i))
            for h in range(GROUP):
                part = slice(h * ROWS, (h + 1) * ROWS)
                blocks = [slice(base + c * ROWS, base + (c + 1) * ROWS) for c in range(i + 1)]
                diagonal = jnp.where(tri, raised[kv, blocks[i], part], -1e30)
                top = diagonal
                for c in range(i):
                    top = jnp.maximum(top, raised[kv, blocks[c], part])
                top = jnp.max(top, axis=0, keepdims=True)
                total = jnp.zeros((ROWS, ROWS), F32)
                center = jnp.zeros((ROWS, ROWS), F32)
                for c in range(i + 1):
                    piece = diagonal if c == i else raised[kv, blocks[c], part]
                    piece = jnp.exp2((piece - top) * LOG2)
                    raised[kv, blocks[c], part] = piece
                    total = total + piece
                    center = center + piece * dprobs[kv, blocks[c], part]
                stats[kv, i, 0:1, part] = top
                stats[kv, i, 1:2, part] = jnp.sum(total, axis=0, keepdims=True)
                stats[kv, i, 2:3, part] = jnp.sum(center, axis=0, keepdims=True)
        return carry

    def prompt_part(kv, carry):
        front_k = rows[:PLEN, lanes(kv)]
        front_v = rows[PLEN:, lanes(kv)]
        term_k = jnp.zeros((PLEN, HD), F32)
        term_v = jnp.zeros((PLEN, HD), F32)
        for i in range(TILES):
            query = stacked(q_buf, kv, i)
            grad = stacked(g_buf, kv, i)
            scores = dot_nt(front_k, query)
            first_dp = dot_nt(front_v, grad)
            live = row_at + i * ROWS < length
            for h in range(GROUP):
                part = slice(h * ROWS, (h + 1) * ROWS)
                own_top = stats[kv, i, 0:1, part]
                top = jnp.maximum(jnp.max(scores[:, part], axis=0, keepdims=True), own_top)
                alpha = jnp.exp2((own_top - top) * LOG2)
                first_e = jnp.exp2((scores[:, part] - top) * LOG2)
                dp = first_dp[:, part]
                total = alpha * stats[kv, i, 1:2, part] + jnp.sum(first_e, axis=0, keepdims=True)
                center = alpha * stats[kv, i, 2:3, part] + jnp.sum(first_e * dp, axis=0, keepdims=True)
                inv = 1.0 / total
                center = center * inv
                inv = jnp.where(live, inv, 0.0)
                stats[kv, i, 3:4, part] = alpha * inv
                stats[kv, i, 4:5, part] = center
                probs = first_e * inv
                front_p[kv, i, :, part] = probs.astype(BF16)
                front_d[kv, i, :, part] = (probs * ((dp - center) * SCALE)).astype(BF16)
            term_k = term_k + dot_nn(front_d[kv, i], query)
            term_v = term_v + dot_nn(front_p[kv, i], grad)
        terms[:PLEN, lanes(kv)] = term_k.astype(BF16)
        terms[PLEN:, lanes(kv)] = term_v.astype(BF16)
        return carry

    def own_backward(kv, carry):
        front_k = rows[:PLEN, lanes(kv)]
        front_v = rows[PLEN:, lanes(kv)]
        sum_k[...] = jnp.zeros_like(sum_k)
        sum_v[...] = jnp.zeros_like(sum_v)
        for i in range(TILES):
            seen = (i + 1) * ROWS
            base = STARTS[i]
            query = stacked(q_buf, kv, i)
            grad = stacked(g_buf, kv, i)
            for h in range(GROUP):
                part = slice(h * ROWS, (h + 1) * ROWS)
                factor = stats[kv, i, 3:4, part]
                center = stats[kv, i, 4:5, part]
                for c in range(i + 1):
                    at = slice(base + c * ROWS, base + (c + 1) * ROWS)
                    probs = raised[kv, at, part] * factor
                    low_p[at, part] = probs.astype(BF16)
                    low_d[at, part] = (probs * ((dprobs[kv, at, part] - center) * SCALE)).astype(BF16)
            own_p = low_p[base : base + seen]
            own_d = low_d[base : base + seen]
            sum_k[:seen] += dot_nn(own_d, query)
            sum_v[:seen] += dot_nn(own_p, grad)
            result = dot_tn(
                jnp.concatenate([front_p[kv, i], own_p], 0), jnp.concatenate([front_v, v_own[:seen, lanes(kv)]], 0)
            )
            grad_q = dot_tn(
                jnp.concatenate([front_d[kv, i], own_d], 0), jnp.concatenate([front_k, k_own[:seen, lanes(kv)]], 0)
            )
            for h in range(GROUP):
                part = slice(h * ROWS, (h + 1) * ROWS)
                out_ref[i * ROWS : (i + 1) * ROWS, head_lanes(kv, h)] = result[part].astype(BF16)
                dq_ref[i * ROWS : (i + 1) * ROWS, head_lanes(kv, h)] = grad_q[part].astype(BF16)
        order = pairs()
        for c in range(TILES):
            at = slice(c * ROWS, (c + 1) * ROWS)
            mixed = dot_tn(order, jnp.concatenate([sum_k[at].astype(BF16), sum_v[at].astype(BF16)], 0))
            dkv_ref[at, :, lanes(kv)] = mixed.astype(BF16).reshape(ROWS, 2, HD)
        return carry

    def run(step, low, high):
        lax.fori_loop(low, high, step, 0)

    cache[...] = cache_ref[...].reshape(cache.shape)

    def first_copy(o):
        return plane_copy(
            grid,
            o,
            lambda peer: cache.at[
                :, pl.ds(pl.multiple_of(lax.rem(peer, grid.nt) * width, width), width)
            ],
            chunk(first, grid.c1),
            send_1,
            recv_1,
        )

    def mark_copy(o):
        return column_copy(grid, o, lambda peer: mark, chunk(marks, grid.c2), send_m, recv_m)

    def second_copy(o):
        return column_copy(grid, o, chunk(chosen, grid.c2), chunk(second, grid.c2), send_2, recv_2)

    def third_copy(part):
        return lambda o: column_copy(
            grid,
            o,
            chunk(outgoing.at[part], grid.c2),
            chunk(third.at[part], grid.c2),
            send_3.at[part],
            recv_3.at[part],
        )

    def fourth_copy(part):
        return lambda o: plane_copy(
            grid,
            o,
            chunk(dense.at[part], grid.c1),
            chunk(fourth.at[part], grid.c1),
            send_4.at[part],
            recv_4.at[part],
        )

    in_plane = pl.ds(pl.multiple_of(u * grid.c1, grid.c1), grid.c1)
    in_column = pl.ds(pl.multiple_of(b * grid.c2, grid.c2), grid.c2)

    def send_terms(part):
        outgoing[part] = dot_tn(shuffle(grid), terms[:, part * half : (part + 1) * half]).astype(BF16)
        start_all(third_copy(part), grid.nb)
        third[part, in_column] = outgoing[part, in_column]

    def send_sums(part):
        wait_recv_all(third_copy(part), grid.nb)
        dense[part] = dot_tn(pick[...], third[part]).astype(BF16)
        start_all(fourth_copy(part), grid.nu)
        fourth[part, in_plane] = dense[part, in_plane]

    def finish(part):
        wait_recv_all(fourth_copy(part), grid.nu)
        for at_t in range(grid.nt):
            total = jnp.zeros((grid.c1, half), F32)
            for at in range(at_t, grid.nu, grid.nt):
                total = total + fourth[part, at * grid.c1 : (at + 1) * grid.c1].astype(F32)
            cgrad_ref[:, :, at_t * width + part * half : at_t * width + (part + 1) * half] = total.astype(
                BF16
            ).reshape(grid.bl, 2, half)

    def load_all(kv, carry):
        load_q(kv).start()
        load_g(kv).start()
        return carry

    run(load_all, 0, heads)
    block = jnp.int32(0)
    for i in range(order_ref.shape[0]):
        block = block + jnp.where(order_ref[i] == owner_ref[0], i, 0)
    mark[...] = jnp.full(mark.shape, block.astype(F32), F32)
    greet(grid)
    start_all(first_copy, grid.nu)
    start_all(mark_copy, grid.nb)
    first[in_plane] = cache[:, pl.ds(pl.multiple_of(t * width, width), width)]
    marks[in_column] = mark[...]
    order = pairs()
    for j in range(TILES):
        split = dot_nn(order, kv_ref[j * ROWS : (j + 1) * ROWS].reshape(2 * ROWS, width)).astype(BF16)
        k_own[j * ROWS : (j + 1) * ROWS] = split[:ROWS]
        v_own[j * ROWS : (j + 1) * ROWS] = split[ROWS:]
    run(own_forward, 0, 2)
    wait_recv_all(mark_copy, grid.nb)
    many = grid.nu * grid.c1 // marks.shape[1]
    pick[...] = choice(
        grid, jnp.concatenate([marks[...]] * many, 1) if many > 1 else marks[:, : grid.nu * grid.c1]
    )
    wait_recv_all(first_copy, grid.nu)
    chosen[...] = dot_nn(pick[...], first[...]).astype(BF16)
    start_all(second_copy, grid.nb)
    second[in_column] = chosen[in_column]
    run(own_forward, 2, heads)
    wait_recv_all(second_copy, grid.nb)
    rows[...] = dot_nn(shuffle(grid), second[...]).astype(BF16)
    run(prompt_part, 0, heads // 2)
    send_terms(0)
    run(prompt_part, heads // 2, heads)
    send_terms(1)
    run(own_backward, 0, 1)
    send_sums(0)
    run(own_backward, 1, 2)
    send_sums(1)
    run(own_backward, 2, heads)
    finish(0)
    finish(1)

    wait_send_all(first_copy, grid.nu)
    wait_send_all(mark_copy, grid.nb)
    wait_send_all(second_copy, grid.nb)
    for part in range(2):
        wait_send_all(third_copy(part), grid.nb)
        wait_send_all(fourth_copy(part), grid.nu)


def hand_on(*refs):
    copies = [pltpu.make_async_copy(refs[i], refs[4 + i], refs[8].at[i]) for i in range(4)]
    for copy in copies:
        copy.start()
    for copy in copies:
        copy.wait()


def local(
    grid,
    response_query,
    response_kv,
    prompt_cache,
    prompt_order,
    response_prompt,
    response_length,
    out_grad,
):
    width = response_kv.shape[3]
    heads = width // HD
    half = width // 2
    vmem = pl.BlockSpec(memory_space=pltpu.VMEM)
    smem = pl.BlockSpec(memory_space=pltpu.SMEM)
    hbm = pl.BlockSpec(memory_space=pl.ANY)
    dma = pltpu.SemaphoreType.DMA
    all_rows = grid.nb * grid.c2
    all_blocks = grid.nu * grid.c1
    full = (heads, RMAX, STACK)
    flat = response_query.shape[1:]
    out, dq, dkv, summed = pl.pallas_call(
        functools.partial(kernel, grid),
        out_shape=(
            jax.ShapeDtypeStruct(flat, BF16),
            jax.ShapeDtypeStruct(flat, BF16),
            jax.ShapeDtypeStruct((RMAX, 2, width), BF16),
            jax.ShapeDtypeStruct((grid.bl, 2, grid.nt * width), BF16),
        ),
        in_specs=[smem] * 3 + [vmem] * 2 + [hbm] * 2,
        out_specs=(vmem,) * 4,
        scratch_shapes=[
            pltpu.VMEM((grid.c1, grid.nt * width), BF16),
            pltpu.VMEM((grid.c2, HD), F32),
            pltpu.VMEM((all_rows, HD), F32),
            pltpu.VMEM((all_blocks, width), BF16),
            pltpu.VMEM((all_rows, all_blocks), BF16),
            pltpu.VMEM((all_rows, width), BF16),
            pltpu.VMEM((all_rows, width), BF16),
            pltpu.VMEM((all_rows, width), BF16),
            pltpu.VMEM((all_rows, width), BF16),
            pltpu.VMEM((2, all_rows, half), BF16),
            pltpu.VMEM((2, all_rows, half), BF16),
            pltpu.VMEM((2, all_blocks, half), BF16),
            pltpu.VMEM((2, all_blocks, half), BF16),
            pltpu.VMEM(full, BF16),
            pltpu.VMEM(full, BF16),
            pltpu.VMEM((RMAX, width), BF16),
            pltpu.VMEM((RMAX, width), BF16),
            pltpu.VMEM((heads, WIDE, STACK), F32),
            pltpu.VMEM((heads, WIDE, STACK), F32),
            pltpu.VMEM((heads, TILES, 8, STACK), F32),
            pltpu.VMEM((heads, TILES, PLEN, STACK), BF16),
            pltpu.VMEM((heads, TILES, PLEN, STACK), BF16),
            pltpu.VMEM((WIDE, STACK), BF16),
            pltpu.VMEM((WIDE, STACK), BF16),
            pltpu.VMEM((RMAX, HD), F32),
            pltpu.VMEM((RMAX, HD), F32),
            dma((2, heads)),
            dma((grid.nb,)),
            dma((grid.nb,)),
            dma((grid.nu,)),
            dma((grid.nu,)),
            dma((grid.nb,)),
            dma((grid.nb,)),
            dma((2, grid.nb)),
            dma((2, grid.nb)),
            dma((2, grid.nu)),
            dma((2, grid.nu)),
        ],
        compiler_params=pltpu.CompilerParams(
            collective_id=0, has_side_effects=True, vmem_limit_bytes=46 * 1024 * 1024
        ),
    )(
        prompt_order,
        response_prompt,
        response_length,
        prompt_cache[0],
        response_kv[0],
        response_query[0],
        out_grad[0],
    )
    out, dq, dkv, summed = pl.pallas_call(
        hand_on,
        out_shape=tuple(jax.ShapeDtypeStruct(x.shape, x.dtype) for x in (out, dq, dkv, summed)),
        in_specs=[hbm] * 4,
        out_specs=(hbm,) * 4,
        scratch_shapes=[dma((4,))],
        compiler_params=pltpu.CompilerParams(vmem_limit_bytes=1024 * 1024),
    )(out, dq, dkv, summed)
    return (out[None], dq[None], dkv[None], summed[None])


def solution(mesh):
    grid = Grid(mesh.shape["seq"], mesh.shape["tp"], 16)
    return jax.shard_map(
        functools.partial(local, grid),
        mesh=mesh,
        in_specs=(
            P("seq", None, "tp"),
            P("seq", None, None, "tp"),
            P("seq", "tp", None, None),
            P(),
            P("seq"),
            P("seq"),
            P("seq", None, "tp"),
        ),
        out_specs=(
            P("seq", None, "tp"),
            P("seq", None, "tp"),
            P("seq", None, None, "tp"),
            P("seq", "tp", None, None),
        ),
        check_vma=False,
    )
```

```python
import functools
import math

import jax
import jax.numpy as jnp
from jax import lax
from jax.experimental import pallas as pl
from jax.experimental.pallas import tpu as pltpu
from jax.sharding import PartitionSpec as P

HQ = 40
KVH = 8
HD = 128
PLEN = 128
RMAX = 512
GROUP = HQ // KVH
ROWS = 128
TILES = RMAX // ROWS
STACK = GROUP * ROWS
STARTS = (0, 128, 384, 768)
LOWS = (0, 128, 384, 0)
LOW = 768
WIDE = 1280
SCALE = 1.0 / math.sqrt(HD)
LOG2 = SCALE * math.log2(math.e)
F32 = jnp.float32
BF16 = jnp.bfloat16
MESH = pl.DeviceIdType.MESH


def dot_nn(a, b):
    return lax.dot_general(a, b, (((1,), (0,)), ((), ())), preferred_element_type=F32)


def dot_nt(a, b):
    return lax.dot_general(a, b, (((1,), (1,)), ((), ())), preferred_element_type=F32)


def dot_tn(a, b):
    return lax.dot_general(a, b, (((0,), (0,)), ((), ())), preferred_element_type=F32)


class Grid:
    def __init__(self, seq, tp, blocks):
        self.nb = 16 if seq >= 128 else 4
        self.na = seq // self.nb
        self.nt = tp
        self.nu = self.na * tp
        self.bl = blocks // tp
        self.c1 = self.bl * 2
        self.c2 = self.na * 2

    def here(self):
        seq, t = lax.axis_index("seq"), lax.axis_index("tp")
        a, b = seq // self.nb, lax.rem(seq, self.nb)
        return a, b, t, a * self.nt + t

    def plane(self, u, b):
        return {"seq": (u // self.nt) * self.nb + b, "tp": lax.rem(u, self.nt)}

    def column(self, a, b, t):
        return {"seq": a * self.nb + b, "tp": t}


def greet(grid):
    a, b, t, u = grid.here()
    barrier = pltpu.get_barrier_semaphore()

    def plane(o, carry):
        peer = lax.rem(u + o, grid.nu)
        pl.semaphore_signal(barrier, inc=1, device_id=grid.plane(peer, b), device_id_type=MESH)
        return carry

    def column(o, carry):
        peer = lax.rem(b + o, grid.nb)
        pl.semaphore_signal(barrier, inc=1, device_id=grid.column(a, peer, t), device_id_type=MESH)
        return carry

    lax.fori_loop(1, grid.nu, plane, 0)
    lax.fori_loop(1, grid.nb, column, 0)
    pl.semaphore_wait(barrier, grid.nu + grid.nb - 2)


def plane_copy(grid, o, source, target, send, recv):
    a, b, t, u = grid.here()
    peer = lax.rem(u + o, grid.nu)
    return pltpu.make_async_remote_copy(
        src_ref=source(peer),
        dst_ref=target(u),
        send_sem=send.at[o],
        recv_sem=recv.at[o],
        device_id=grid.plane(peer, b),
        device_id_type=MESH,
    )


def column_copy(grid, o, source, target, send, recv):
    a, b, t, u = grid.here()
    peer = lax.rem(b + o, grid.nb)
    return pltpu.make_async_remote_copy(
        src_ref=source(peer),
        dst_ref=target(b),
        send_sem=send.at[o],
        recv_sem=recv.at[o],
        device_id=grid.column(a, peer, t),
        device_id_type=MESH,
    )


def start_all(copy, count):
    def step(o, carry):
        copy(o).start()
        return carry

    lax.fori_loop(1, count, step, 0)


def wait_recv_all(copy, count):
    def step(o, carry):
        copy(o).wait_recv()
        return carry

    lax.fori_loop(1, count, step, 0)


def wait_send_all(copy, count):
    def step(o, carry):
        copy(o).wait_send()
        return carry

    lax.fori_loop(1, count, step, 0)


def chunk(ref, size):
    return lambda i: ref.at[pl.ds(pl.multiple_of(i * size, size), size)]


def choice(grid, picks):
    rows, cols = grid.nb * grid.c2, grid.nu * grid.c1
    row = lax.broadcasted_iota(jnp.int32, (rows, cols), 0)
    col = lax.broadcasted_iota(jnp.int32, (rows, cols), 1)
    inner = row % grid.c2
    kv, a = inner // grid.na, inner % grid.na
    wanted = a * (grid.nt * grid.c1) + picks.astype(jnp.int32) * 2 + kv
    return jnp.where(col == wanted, 1.0, 0.0).astype(BF16)


def shuffle(grid):
    rows = grid.nb * grid.c2
    row = lax.broadcasted_iota(jnp.int32, (rows, rows), 0)
    col = lax.broadcasted_iota(jnp.int32, (rows, rows), 1)
    half = grid.nb * grid.na
    kv, b, a = row // half, (row % half) // grid.na, row % grid.na
    return jnp.where(col == b * grid.c2 + kv * grid.na + a, 1.0, 0.0).astype(BF16)


def pairs():
    row = lax.broadcasted_iota(jnp.int32, (2 * ROWS, 2 * ROWS), 0)
    col = lax.broadcasted_iota(jnp.int32, (2 * ROWS, 2 * ROWS), 1)
    return jnp.where(col == (row % ROWS) * 2 + row // ROWS, 1.0, 0.0).astype(BF16)


def kernel(
    grid,
    order_ref,
    owner_ref,
    length_ref,
    cache_ref,
    kv_ref,
    q_hbm,
    g_hbm,
    out_ref,
    dq_ref,
    dkv_ref,
    cgrad_ref,
    cache,
    mark,
    marks,
    first,
    pick,
    chosen,
    second,
    rows,
    terms,
    outgoing,
    third,
    dense,
    fourth,
    q_buf,
    g_buf,
    k_own,
    v_own,
    scores,
    memo_o,
    raised,
    dprobs,
    stats,
    front_p,
    front_d,
    low_p,
    low_d,
    sum_k,
    sum_v,
    in_sem,
    send_m,
    recv_m,
    send_1,
    recv_1,
    send_2,
    recv_2,
    send_3,
    recv_3,
    send_4,
    recv_4,
):
    a, b, t, u = grid.here()
    heads = q_buf.shape[0]
    width = k_own.shape[1]
    half = width // 2
    length = length_ref[0]

    def moved(kv):
        return pl.ds(pl.multiple_of(kv * STACK, STACK), STACK)

    def load_q(kv):
        return pltpu.make_async_copy(q_hbm.at[:, moved(kv)], q_buf.at[kv], in_sem.at[0, kv])

    def load_g(kv):
        return pltpu.make_async_copy(g_hbm.at[:, moved(kv)], g_buf.at[kv], in_sem.at[1, kv])

    def stacked(ref, kv, i):
        return jnp.concatenate(
            [ref[kv, i * ROWS : (i + 1) * ROWS, h * HD : (h + 1) * HD] for h in range(GROUP)], 0
        )

    def lanes(kv):
        return pl.ds(pl.multiple_of(kv * HD, HD), HD)

    def head_lanes(kv, h):
        return pl.ds(pl.multiple_of(kv * STACK + h * HD, HD), HD)

    tri = lax.broadcasted_iota(jnp.int32, (ROWS, ROWS), 0) <= lax.broadcasted_iota(jnp.int32, (ROWS, ROWS), 1)
    row_at = lax.broadcasted_iota(jnp.int32, (1, ROWS), 1)

    def own_forward(kv, carry):
        load_q(kv).wait()
        load_g(kv).wait()
        for i in range(TILES):
            seen = (i + 1) * ROWS
            base = STARTS[i]
            scores[LOWS[i] : LOWS[i] + seen] = dot_nt(k_own[:seen, lanes(kv)], stacked(q_buf, kv, i))
            dprobs[kv, base : base + seen] = dot_nt(v_own[:seen, lanes(kv)], stacked(g_buf, kv, i))
            for h in range(GROUP):
                part = slice(h * ROWS, (h + 1) * ROWS)
                blocks = [slice(base + c * ROWS, base + (c + 1) * ROWS) for c in range(i + 1)]
                diagonal = jnp.where(tri, scores[LOWS[i] + i * ROWS : LOWS[i] + (i + 1) * ROWS, part], -1e30)
                top = diagonal
                for c in range(i):
                    top = jnp.maximum(top, scores[LOWS[i] + c * ROWS : LOWS[i] + (c + 1) * ROWS, part])
                top = jnp.max(top, axis=0, keepdims=True)
                total = jnp.zeros((ROWS, ROWS), F32)
                center = jnp.zeros((ROWS, ROWS), F32)
                for c in range(i + 1):
                    piece = diagonal if c == i else scores[LOWS[i] + c * ROWS : LOWS[i] + (c + 1) * ROWS, part]
                    piece = jnp.exp2((piece - top) * LOG2)
                    raised[kv, blocks[c], part] = piece.astype(BF16)
                    total = total + piece
                    center = center + piece * dprobs[kv, blocks[c], part]
                stats[kv, i, 0:1, part] = top
                stats[kv, i, 1:2, part] = jnp.sum(total, axis=0, keepdims=True)
                stats[kv, i, 2:3, part] = jnp.sum(center, axis=0, keepdims=True)
            memo_o[kv, i] = dot_tn(v_own[:seen, lanes(kv)], raised[kv, base : base + seen]).astype(BF16)
        return carry

    def prompt_part(kv, carry):
        front_k = rows[:PLEN, lanes(kv)]
        front_v = rows[PLEN:, lanes(kv)]
        term_k = jnp.zeros((PLEN, HD), F32)
        term_v = jnp.zeros((PLEN, HD), F32)
        for i in range(TILES):
            query = stacked(q_buf, kv, i)
            grad = stacked(g_buf, kv, i)
            scores = dot_nt(front_k, query)
            first_dp = dot_nt(front_v, grad)
            live = row_at + i * ROWS < length
            for h in range(GROUP):
                part = slice(h * ROWS, (h + 1) * ROWS)
                own_top = stats[kv, i, 0:1, part]
                top = jnp.maximum(jnp.max(scores[:, part], axis=0, keepdims=True), own_top)
                alpha = jnp.exp2((own_top - top) * LOG2)
                first_e = jnp.exp2((scores[:, part] - top) * LOG2)
                dp = first_dp[:, part]
                total = alpha * stats[kv, i, 1:2, part] + jnp.sum(first_e, axis=0, keepdims=True)
                center = alpha * stats[kv, i, 2:3, part] + jnp.sum(first_e * dp, axis=0, keepdims=True)
                inv = 1.0 / total
                center = center * inv
                inv = jnp.where(live, inv, 0.0)
                stats[kv, i, 3:4, part] = alpha * inv
                stats[kv, i, 4:5, part] = center
                probs = first_e * inv
                front_p[kv, i, :, part] = probs.astype(BF16)
                front_d[kv, i, :, part] = (probs * ((dp - center) * SCALE)).astype(BF16)
            term_k = term_k + dot_nn(front_d[kv, i], query)
            term_v = term_v + dot_nn(front_p[kv, i], grad)
        terms[:PLEN, lanes(kv)] = term_k.astype(BF16)
        terms[PLEN:, lanes(kv)] = term_v.astype(BF16)
        return carry

    def own_backward(kv, carry):
        front_k = rows[:PLEN, lanes(kv)]
        front_v = rows[PLEN:, lanes(kv)]
        sum_k[...] = jnp.zeros_like(sum_k)
        sum_v[...] = jnp.zeros_like(sum_v)
        for i in range(TILES):
            seen = (i + 1) * ROWS
            base = STARTS[i]
            query = stacked(q_buf, kv, i)
            grad = stacked(g_buf, kv, i)
            for h in range(GROUP):
                part = slice(h * ROWS, (h + 1) * ROWS)
                factor = stats[kv, i, 3:4, part]
                center = stats[kv, i, 4:5, part]
                for c in range(i + 1):
                    at = slice(base + c * ROWS, base + (c + 1) * ROWS)
                    probs = raised[kv, at, part].astype(F32) * factor
                    low = slice(LOWS[i] + c * ROWS, LOWS[i] + (c + 1) * ROWS)
                    low_p[low, part] = probs.astype(BF16)
                    low_d[low, part] = (probs * ((dprobs[kv, at, part] - center) * SCALE)).astype(BF16)
            own_p = low_p[LOWS[i] : LOWS[i] + seen]
            own_d = low_d[LOWS[i] : LOWS[i] + seen]
            sum_k[:seen] += dot_nn(own_d, query)
            sum_v[:seen] += dot_nn(own_p, grad)
            result = memo_o[kv, i].astype(F32) * stats[kv, i, 3:4] + dot_tn(front_v, front_p[kv, i])
            grad_q = dot_tn(
                jnp.concatenate([front_k, k_own[:seen, lanes(kv)]], 0), jnp.concatenate([front_d[kv, i], own_d], 0)
            )
            for h in range(GROUP):
                part = slice(h * ROWS, (h + 1) * ROWS)
                out_ref[i * ROWS : (i + 1) * ROWS, head_lanes(kv, h)] = result[:, part].T.astype(BF16)
                dq_ref[i * ROWS : (i + 1) * ROWS, head_lanes(kv, h)] = grad_q[:, part].T.astype(BF16)
        order = pairs()
        for c in range(TILES):
            at = slice(c * ROWS, (c + 1) * ROWS)
            mixed = dot_tn(order, jnp.concatenate([sum_k[at].astype(BF16), sum_v[at].astype(BF16)], 0))
            dkv_ref[at, :, lanes(kv)] = mixed.astype(BF16).reshape(ROWS, 2, HD)
        return carry

    def run(step, low, high):
        lax.fori_loop(low, high, step, 0)

    cache[...] = cache_ref[...].reshape(cache.shape)

    def side(at_t, part):
        return pl.ds(pl.multiple_of(at_t * width + part * half, half), half)

    def first_copy(part):
        return lambda o: plane_copy(
            grid,
            o,
            lambda peer: cache.at[:, side(lax.rem(peer, grid.nt), part)],
            chunk(first.at[part], grid.c1),
            send_1.at[part],
            recv_1.at[part],
        )

    def mark_copy(o):
        return column_copy(grid, o, lambda peer: mark, chunk(marks, grid.c2), send_m, recv_m)

    def second_copy(part):
        return lambda o: column_copy(
            grid,
            o,
            chunk(chosen.at[part], grid.c2),
            chunk(second.at[part], grid.c2),
            send_2.at[part],
            recv_2.at[part],
        )

    def third_copy(part):
        return lambda o: column_copy(
            grid,
            o,
            chunk(outgoing.at[part], grid.c2),
            chunk(third.at[part], grid.c2),
            send_3.at[part],
            recv_3.at[part],
        )

    def fourth_copy(part):
        return lambda o: plane_copy(
            grid,
            o,
            chunk(dense.at[part], grid.c1),
            chunk(fourth.at[part], grid.c1),
            send_4.at[part],
            recv_4.at[part],
        )

    in_plane = pl.ds(pl.multiple_of(u * grid.c1, grid.c1), grid.c1)
    in_column = pl.ds(pl.multiple_of(b * grid.c2, grid.c2), grid.c2)

    def send_rows(part):
        wait_recv_all(first_copy(part), grid.nu)
        chosen[part] = dot_nn(pick[...], first[part]).astype(BF16)
        start_all(second_copy(part), grid.nb)
        second[part, in_column] = chosen[part, in_column]

    def take_rows(part):
        wait_recv_all(second_copy(part), grid.nb)
        rows[:, part * half : (part + 1) * half] = dot_nn(shuffle(grid), second[part]).astype(BF16)

    def send_terms(part):
        outgoing[part] = dot_tn(shuffle(grid), terms[:, part * half : (part + 1) * half]).astype(BF16)
        start_all(third_copy(part), grid.nb)
        third[part, in_column] = outgoing[part, in_column]

    def send_sums(part):
        wait_recv_all(third_copy(part), grid.nb)
        dense[part] = dot_tn(pick[...], third[part]).astype(BF16)
        start_all(fourth_copy(part), grid.nu)
        fourth[part, in_plane] = dense[part, in_plane]

    def finish(part):
        wait_recv_all(fourth_copy(part), grid.nu)
        for at_t in range(grid.nt):
            total = jnp.zeros((grid.c1, half), F32)
            for at in range(at_t, grid.nu, grid.nt):
                total = total + fourth[part, at * grid.c1 : (at + 1) * grid.c1].astype(F32)
            cgrad_ref[:, :, at_t * width + part * half : at_t * width + (part + 1) * half] = total.astype(
                BF16
            ).reshape(grid.bl, 2, half)

    def load_all(kv, carry):
        load_q(kv).start()
        load_g(kv).start()
        return carry

    run(load_all, 0, heads)
    block = jnp.int32(0)
    for i in range(order_ref.shape[0]):
        block = block + jnp.where(order_ref[i] == owner_ref[0], i, 0)
    mark[...] = jnp.full(mark.shape, block.astype(F32), F32)
    greet(grid)
    start_all(first_copy(0), grid.nu)
    start_all(mark_copy, grid.nb)
    start_all(first_copy(1), grid.nu)
    for part in range(2):
        first[part, in_plane] = cache[:, side(t, part)]
    marks[in_column] = mark[...]
    order = pairs()
    for j in range(TILES):
        split = dot_nn(order, kv_ref[j * ROWS : (j + 1) * ROWS].reshape(2 * ROWS, width)).astype(BF16)
        k_own[j * ROWS : (j + 1) * ROWS] = split[:ROWS]
        v_own[j * ROWS : (j + 1) * ROWS] = split[ROWS:]
    run(own_forward, 0, 2)
    wait_recv_all(mark_copy, grid.nb)
    many = grid.nu * grid.c1 // marks.shape[1]
    pick[...] = choice(
        grid, jnp.concatenate([marks[...]] * many, 1) if many > 1 else marks[:, : grid.nu * grid.c1]
    )
    send_rows(0)
    run(own_forward, 2, 3)
    send_rows(1)
    run(own_forward, 3, heads)
    take_rows(0)
    run(prompt_part, 0, heads // 2)
    send_terms(0)
    take_rows(1)
    run(prompt_part, heads // 2, heads)
    send_terms(1)
    run(own_backward, 0, 1)
    send_sums(0)
    run(own_backward, 1, 2)
    send_sums(1)
    run(own_backward, 2, heads)
    finish(0)
    finish(1)

    wait_send_all(mark_copy, grid.nb)
    for part in range(2):
        wait_send_all(first_copy(part), grid.nu)
        wait_send_all(second_copy(part), grid.nb)
        wait_send_all(third_copy(part), grid.nb)
        wait_send_all(fourth_copy(part), grid.nu)


def hand_on(*refs):
    copies = [pltpu.make_async_copy(refs[i], refs[4 + i], refs[8].at[i]) for i in range(4)]
    for copy in copies:
        copy.start()
    for copy in copies:
        copy.wait()


def local(
    grid,
    response_query,
    response_kv,
    prompt_cache,
    prompt_order,
    response_prompt,
    response_length,
    out_grad,
):
    width = response_kv.shape[3]
    heads = width // HD
    half = width // 2
    vmem = pl.BlockSpec(memory_space=pltpu.VMEM)
    smem = pl.BlockSpec(memory_space=pltpu.SMEM)
    hbm = pl.BlockSpec(memory_space=pl.ANY)
    dma = pltpu.SemaphoreType.DMA
    all_rows = grid.nb * grid.c2
    all_blocks = grid.nu * grid.c1
    full = (heads, RMAX, STACK)
    flat = response_query.shape[1:]
    out, dq, dkv, summed = pl.pallas_call(
        functools.partial(kernel, grid),
        out_shape=(
            jax.ShapeDtypeStruct(flat, BF16),
            jax.ShapeDtypeStruct(flat, BF16),
            jax.ShapeDtypeStruct((RMAX, 2, width), BF16),
            jax.ShapeDtypeStruct((grid.bl, 2, grid.nt * width), BF16),
        ),
        in_specs=[smem] * 3 + [vmem] * 2 + [hbm] * 2,
        out_specs=(vmem,) * 4,
        scratch_shapes=[
            pltpu.VMEM((grid.c1, grid.nt * width), BF16),
            pltpu.VMEM((grid.c2, HD), F32),
            pltpu.VMEM((all_rows, HD), F32),
            pltpu.VMEM((2, all_blocks, half), BF16),
            pltpu.VMEM((all_rows, all_blocks), BF16),
            pltpu.VMEM((2, all_rows, half), BF16),
            pltpu.VMEM((2, all_rows, half), BF16),
            pltpu.VMEM((all_rows, width), BF16),
            pltpu.VMEM((all_rows, width), BF16),
            pltpu.VMEM((2, all_rows, half), BF16),
            pltpu.VMEM((2, all_rows, half), BF16),
            pltpu.VMEM((2, all_blocks, half), BF16),
            pltpu.VMEM((2, all_blocks, half), BF16),
            pltpu.VMEM(full, BF16),
            pltpu.VMEM(full, BF16),
            pltpu.VMEM((RMAX, width), BF16),
            pltpu.VMEM((RMAX, width), BF16),
            pltpu.VMEM((LOW, STACK), F32),
            pltpu.VMEM((heads, TILES, HD, STACK), BF16),
            pltpu.VMEM((heads, WIDE, STACK), BF16),
            pltpu.VMEM((heads, WIDE, STACK), F32),
            pltpu.VMEM((heads, TILES, 8, STACK), F32),
            pltpu.VMEM((heads, TILES, PLEN, STACK), BF16),
            pltpu.VMEM((heads, TILES, PLEN, STACK), BF16),
            pltpu.VMEM((LOW, STACK), BF16),
            pltpu.VMEM((LOW, STACK), BF16),
            pltpu.VMEM((RMAX, HD), F32),
            pltpu.VMEM((RMAX, HD), F32),
            dma((2, heads)),
            dma((grid.nb,)),
            dma((grid.nb,)),
            dma((2, grid.nu)),
            dma((2, grid.nu)),
            dma((2, grid.nb)),
            dma((2, grid.nb)),
            dma((2, grid.nb)),
            dma((2, grid.nb)),
            dma((2, grid.nu)),
            dma((2, grid.nu)),
        ],
        compiler_params=pltpu.CompilerParams(
            collective_id=0, has_side_effects=True, vmem_limit_bytes=46 * 1024 * 1024
        ),
    )(
        prompt_order,
        response_prompt,
        response_length,
        prompt_cache[0],
        response_kv[0],
        response_query[0],
        out_grad[0],
    )
    out, dq, dkv, summed = pl.pallas_call(
        hand_on,
        out_shape=tuple(jax.ShapeDtypeStruct(x.shape, x.dtype) for x in (out, dq, dkv, summed)),
        in_specs=[hbm] * 4,
        out_specs=(hbm,) * 4,
        scratch_shapes=[dma((4,))],
        compiler_params=pltpu.CompilerParams(vmem_limit_bytes=1024 * 1024),
    )(out, dq, dkv, summed)
    return (out[None], dq[None], dkv[None], summed[None])


def solution(mesh):
    grid = Grid(mesh.shape["seq"], mesh.shape["tp"], 16)
    return jax.shard_map(
        functools.partial(local, grid),
        mesh=mesh,
        in_specs=(
            P("seq", None, "tp"),
            P("seq", None, None, "tp"),
            P("seq", "tp", None, None),
            P(),
            P("seq"),
            P("seq"),
            P("seq", None, "tp"),
        ),
        out_specs=(
            P("seq", None, "tp"),
            P("seq", None, "tp"),
            P("seq", None, None, "tp"),
            P("seq", "tp", None, None),
        ),
        check_vma=False,
    )
```

```python
import functools
import math

import jax
import jax.numpy as jnp
from jax import lax
from jax.experimental import pallas as pl
from jax.experimental.pallas import tpu as pltpu
from jax.sharding import PartitionSpec as P

HQ = 40
KVH = 8
HD = 128
PLEN = 128
RMAX = 512
GROUP = HQ // KVH
ROWS = 128
TILES = RMAX // ROWS
STACK = GROUP * ROWS
STARTS = (0, 128, 384, 768)
LOWS = (0, 128, 384, 0)
LOW = 768
WIDE = 1280
SCALE = 1.0 / math.sqrt(HD)
LOG2 = SCALE * math.log2(math.e)
F32 = jnp.float32
BF16 = jnp.bfloat16
MESH = pl.DeviceIdType.MESH


def dot_nn(a, b):
    return lax.dot_general(a, b, (((1,), (0,)), ((), ())), preferred_element_type=F32)


def dot_nt(a, b):
    return lax.dot_general(a, b, (((1,), (1,)), ((), ())), preferred_element_type=F32)


def dot_tn(a, b):
    return lax.dot_general(a, b, (((0,), (0,)), ((), ())), preferred_element_type=F32)


class Grid:
    def __init__(self, seq, tp, blocks):
        self.nb = 16 if seq >= 128 else 4
        self.na = seq // self.nb
        self.nt = tp
        self.nu = self.na * tp
        self.bl = blocks // tp
        self.c1 = self.bl * 2
        self.c2 = self.na * 2

    def here(self):
        seq, t = lax.axis_index("seq"), lax.axis_index("tp")
        a, b = seq // self.nb, lax.rem(seq, self.nb)
        return a, b, t, a * self.nt + t

    def plane(self, u, b):
        return {"seq": (u // self.nt) * self.nb + b, "tp": lax.rem(u, self.nt)}

    def column(self, a, b, t):
        return {"seq": a * self.nb + b, "tp": t}


def greet(grid):
    a, b, t, u = grid.here()
    barrier = pltpu.get_barrier_semaphore()

    def plane(o, carry):
        peer = lax.rem(u + o, grid.nu)
        pl.semaphore_signal(barrier, inc=1, device_id=grid.plane(peer, b), device_id_type=MESH)
        return carry

    def column(o, carry):
        peer = lax.rem(b + o, grid.nb)
        pl.semaphore_signal(barrier, inc=1, device_id=grid.column(a, peer, t), device_id_type=MESH)
        return carry

    lax.fori_loop(1, grid.nu, plane, 0)
    lax.fori_loop(1, grid.nb, column, 0)
    pl.semaphore_wait(barrier, grid.nu + grid.nb - 2)


def plane_copy(grid, o, source, target, send, recv):
    a, b, t, u = grid.here()
    peer = lax.rem(u + o, grid.nu)
    return pltpu.make_async_remote_copy(
        src_ref=source(peer),
        dst_ref=target(u),
        send_sem=send.at[o],
        recv_sem=recv.at[o],
        device_id=grid.plane(peer, b),
        device_id_type=MESH,
    )


def column_copy(grid, o, source, target, send, recv):
    a, b, t, u = grid.here()
    peer = lax.rem(b + o, grid.nb)
    return pltpu.make_async_remote_copy(
        src_ref=source(peer),
        dst_ref=target(b),
        send_sem=send.at[o],
        recv_sem=recv.at[o],
        device_id=grid.column(a, peer, t),
        device_id_type=MESH,
    )


def start_all(copy, count):
    def step(o, carry):
        copy(o).start()
        return carry

    lax.fori_loop(1, count, step, 0)


def wait_recv_all(copy, count):
    def step(o, carry):
        copy(o).wait_recv()
        return carry

    lax.fori_loop(1, count, step, 0)


def wait_send_all(copy, count):
    def step(o, carry):
        copy(o).wait_send()
        return carry

    lax.fori_loop(1, count, step, 0)


def chunk(ref, size):
    return lambda i: ref.at[pl.ds(pl.multiple_of(i * size, size), size)]


def choice(grid, picks):
    rows, cols = grid.nb * grid.c2, grid.nu * grid.c1
    row = lax.broadcasted_iota(jnp.int32, (rows, cols), 0)
    col = lax.broadcasted_iota(jnp.int32, (rows, cols), 1)
    inner = row % grid.c2
    kv, a = inner // grid.na, inner % grid.na
    wanted = a * (grid.nt * grid.c1) + picks.astype(jnp.int32) * 2 + kv
    return jnp.where(col == wanted, 1.0, 0.0).astype(BF16)


def shuffle(grid):
    rows = grid.nb * grid.c2
    row = lax.broadcasted_iota(jnp.int32, (rows, rows), 0)
    col = lax.broadcasted_iota(jnp.int32, (rows, rows), 1)
    half = grid.nb * grid.na
    kv, b, a = row // half, (row % half) // grid.na, row % grid.na
    return jnp.where(col == b * grid.c2 + kv * grid.na + a, 1.0, 0.0).astype(BF16)


def pairs():
    row = lax.broadcasted_iota(jnp.int32, (2 * ROWS, 2 * ROWS), 0)
    col = lax.broadcasted_iota(jnp.int32, (2 * ROWS, 2 * ROWS), 1)
    return jnp.where(col == (row % ROWS) * 2 + row // ROWS, 1.0, 0.0).astype(BF16)


def kernel(
    grid,
    order_ref,
    owner_ref,
    length_ref,
    cache_ref,
    kv_ref,
    q_hbm,
    g_hbm,
    out_ref,
    dq_ref,
    dkv_ref,
    cgrad_ref,
    regroup,
    pairing,
    cache,
    mark,
    marks,
    first,
    pick,
    chosen,
    second,
    rows,
    terms,
    outgoing,
    third,
    dense,
    fourth,
    q_buf,
    g_buf,
    k_own,
    v_own,
    scores,
    memo_o,
    raised,
    dprobs,
    stats,
    front_p,
    front_d,
    low_p,
    low_d,
    sum_k,
    sum_v,
    in_sem,
    send_m,
    recv_m,
    send_1,
    recv_1,
    send_2,
    recv_2,
    send_3,
    recv_3,
    send_4,
    recv_4,
):
    a, b, t, u = grid.here()
    heads = q_buf.shape[0]
    width = k_own.shape[1]
    half = width // 2
    length = length_ref[0]

    def moved(kv):
        return pl.ds(pl.multiple_of(kv * STACK, STACK), STACK)

    def load_q(kv):
        return pltpu.make_async_copy(q_hbm.at[:, moved(kv)], q_buf.at[kv], in_sem.at[0, kv])

    def load_g(kv):
        return pltpu.make_async_copy(g_hbm.at[:, moved(kv)], g_buf.at[kv], in_sem.at[1, kv])

    def stacked(ref, kv, i):
        return jnp.concatenate(
            [ref[kv, i * ROWS : (i + 1) * ROWS, h * HD : (h + 1) * HD] for h in range(GROUP)], 0
        )

    def lanes(kv):
        return pl.ds(pl.multiple_of(kv * HD, HD), HD)

    def head_lanes(kv, h):
        return pl.ds(pl.multiple_of(kv * STACK + h * HD, HD), HD)

    tri = lax.broadcasted_iota(jnp.int32, (ROWS, ROWS), 0) <= lax.broadcasted_iota(jnp.int32, (ROWS, ROWS), 1)
    row_at = lax.broadcasted_iota(jnp.int32, (1, ROWS), 1)

    def own_forward(kv, carry):
        load_q(kv).wait()
        load_g(kv).wait()
        for i in range(TILES):
            seen = (i + 1) * ROWS
            base = STARTS[i]
            scores[LOWS[i] : LOWS[i] + seen] = dot_nt(k_own[:seen, lanes(kv)], stacked(q_buf, kv, i))
            dprobs[kv, base : base + seen] = dot_nt(v_own[:seen, lanes(kv)], stacked(g_buf, kv, i))
            for h in range(GROUP):
                part = slice(h * ROWS, (h + 1) * ROWS)
                blocks = [slice(base + c * ROWS, base + (c + 1) * ROWS) for c in range(i + 1)]
                diagonal = jnp.where(tri, scores[LOWS[i] + i * ROWS : LOWS[i] + (i + 1) * ROWS, part], -1e30)
                top = diagonal
                for c in range(i):
                    top = jnp.maximum(top, scores[LOWS[i] + c * ROWS : LOWS[i] + (c + 1) * ROWS, part])
                top = jnp.max(top, axis=0, keepdims=True)
                total = jnp.zeros((ROWS, ROWS), F32)
                center = jnp.zeros((ROWS, ROWS), F32)
                for c in range(i + 1):
                    piece = diagonal if c == i else scores[LOWS[i] + c * ROWS : LOWS[i] + (c + 1) * ROWS, part]
                    piece = jnp.exp2((piece - top) * LOG2)
                    raised[kv, blocks[c], part] = piece.astype(BF16)
                    total = total + piece
                    center = center + piece * dprobs[kv, blocks[c], part]
                stats[kv, i, 0:1, part] = top
                stats[kv, i, 1:2, part] = jnp.sum(total, axis=0, keepdims=True)
                stats[kv, i, 2:3, part] = jnp.sum(center, axis=0, keepdims=True)
            memo_o[kv, i] = dot_tn(v_own[:seen, lanes(kv)], raised[kv, base : base + seen]).astype(BF16)
        return carry

    def prompt_part(kv, carry):
        front_k = rows[:PLEN, lanes(kv)]
        front_v = rows[PLEN:, lanes(kv)]
        term_k = jnp.zeros((PLEN, HD), F32)
        term_v = jnp.zeros((PLEN, HD), F32)
        for i in range(TILES):
            query = stacked(q_buf, kv, i)
            grad = stacked(g_buf, kv, i)
            scores = dot_nt(front_k, query)
            first_dp = dot_nt(front_v, grad)
            live = row_at + i * ROWS < length
            for h in range(GROUP):
                part = slice(h * ROWS, (h + 1) * ROWS)
                own_top = stats[kv, i, 0:1, part]
                top = jnp.maximum(jnp.max(scores[:, part], axis=0, keepdims=True), own_top)
                alpha = jnp.exp2((own_top - top) * LOG2)
                first_e = jnp.exp2((scores[:, part] - top) * LOG2)
                dp = first_dp[:, part]
                total = alpha * stats[kv, i, 1:2, part] + jnp.sum(first_e, axis=0, keepdims=True)
                center = alpha * stats[kv, i, 2:3, part] + jnp.sum(first_e * dp, axis=0, keepdims=True)
                inv = 1.0 / total
                center = center * inv
                inv = jnp.where(live, inv, 0.0)
                stats[kv, i, 3:4, part] = alpha * inv
                stats[kv, i, 4:5, part] = center
                probs = first_e * inv
                front_p[kv, i, :, part] = probs.astype(BF16)
                front_d[kv, i, :, part] = (probs * ((dp - center) * SCALE)).astype(BF16)
            term_k = term_k + dot_nn(front_d[kv, i], query)
            term_v = term_v + dot_nn(front_p[kv, i], grad)
        terms[:PLEN, lanes(kv)] = term_k.astype(BF16)
        terms[PLEN:, lanes(kv)] = term_v.astype(BF16)
        return carry

    def own_backward(kv, carry):
        front_k = rows[:PLEN, lanes(kv)]
        front_v = rows[PLEN:, lanes(kv)]
        sum_k[...] = jnp.zeros_like(sum_k)
        sum_v[...] = jnp.zeros_like(sum_v)
        for i in range(TILES):
            seen = (i + 1) * ROWS
            base = STARTS[i]
            query = stacked(q_buf, kv, i)
            grad = stacked(g_buf, kv, i)
            for h in range(GROUP):
                part = slice(h * ROWS, (h + 1) * ROWS)
                factor = stats[kv, i, 3:4, part]
                center = stats[kv, i, 4:5, part]
                for c in range(i + 1):
                    at = slice(base + c * ROWS, base + (c + 1) * ROWS)
                    probs = raised[kv, at, part].astype(F32) * factor
                    low = slice(LOWS[i] + c * ROWS, LOWS[i] + (c + 1) * ROWS)
                    low_p[low, part] = probs.astype(BF16)
                    low_d[low, part] = (probs * ((dprobs[kv, at, part] - center) * SCALE)).astype(BF16)
            own_p = low_p[LOWS[i] : LOWS[i] + seen]
            own_d = low_d[LOWS[i] : LOWS[i] + seen]
            sum_k[:seen] += dot_nn(own_d, query)
            sum_v[:seen] += dot_nn(own_p, grad)
            result = memo_o[kv, i].astype(F32) * stats[kv, i, 3:4] + dot_tn(front_v, front_p[kv, i])
            grad_q = dot_tn(
                jnp.concatenate([front_k, k_own[:seen, lanes(kv)]], 0), jnp.concatenate([front_d[kv, i], own_d], 0)
            )
            for h in range(GROUP):
                part = slice(h * ROWS, (h + 1) * ROWS)
                out_ref[i * ROWS : (i + 1) * ROWS, head_lanes(kv, h)] = result[:, part].T.astype(BF16)
                dq_ref[i * ROWS : (i + 1) * ROWS, head_lanes(kv, h)] = grad_q[:, part].T.astype(BF16)
        order = pairing[...]
        for c in range(TILES):
            at = slice(c * ROWS, (c + 1) * ROWS)
            mixed = dot_tn(order, jnp.concatenate([sum_k[at].astype(BF16), sum_v[at].astype(BF16)], 0))
            dkv_ref[at, :, lanes(kv)] = mixed.astype(BF16).reshape(ROWS, 2, HD)
        return carry

    def run(step, low, high):
        lax.fori_loop(low, high, step, 0)

    cache[...] = cache_ref[...].reshape(cache.shape)

    def side(at_t, part):
        return pl.ds(pl.multiple_of(at_t * width + part * half, half), half)

    def first_copy(part):
        return lambda o: plane_copy(
            grid,
            o,
            lambda peer: cache.at[:, side(lax.rem(peer, grid.nt), part)],
            chunk(first.at[part], grid.c1),
            send_1.at[part],
            recv_1.at[part],
        )

    def mark_copy(o):
        return column_copy(grid, o, lambda peer: mark, chunk(marks, grid.c2), send_m, recv_m)

    def second_copy(part):
        return lambda o: column_copy(
            grid,
            o,
            chunk(chosen.at[part], grid.c2),
            chunk(second.at[part], grid.c2),
            send_2.at[part],
            recv_2.at[part],
        )

    def third_copy(part):
        return lambda o: column_copy(
            grid,
            o,
            chunk(outgoing.at[part], grid.c2),
            chunk(third.at[part], grid.c2),
            send_3.at[part],
            recv_3.at[part],
        )

    def fourth_copy(part):
        return lambda o: plane_copy(
            grid,
            o,
            chunk(dense.at[part], grid.c1),
            chunk(fourth.at[part], grid.c1),
            send_4.at[part],
            recv_4.at[part],
        )

    in_plane = pl.ds(pl.multiple_of(u * grid.c1, grid.c1), grid.c1)
    in_column = pl.ds(pl.multiple_of(b * grid.c2, grid.c2), grid.c2)

    def send_rows(part):
        wait_recv_all(first_copy(part), grid.nu)
        chosen[part] = dot_nn(pick[...], first[part]).astype(BF16)
        start_all(second_copy(part), grid.nb)
        second[part, in_column] = chosen[part, in_column]

    def take_rows(part):
        wait_recv_all(second_copy(part), grid.nb)
        rows[:, part * half : (part + 1) * half] = dot_nn(regroup[...], second[part]).astype(BF16)

    def send_terms(part):
        outgoing[part] = dot_tn(regroup[...], terms[:, part * half : (part + 1) * half]).astype(BF16)
        start_all(third_copy(part), grid.nb)
        third[part, in_column] = outgoing[part, in_column]

    def send_sums(part):
        wait_recv_all(third_copy(part), grid.nb)
        dense[part] = dot_tn(pick[...], third[part]).astype(BF16)
        start_all(fourth_copy(part), grid.nu)
        fourth[part, in_plane] = dense[part, in_plane]

    def finish(part):
        wait_recv_all(fourth_copy(part), grid.nu)
        for at_t in range(grid.nt):
            total = jnp.zeros((grid.c1, half), F32)
            for at in range(at_t, grid.nu, grid.nt):
                total = total + fourth[part, at * grid.c1 : (at + 1) * grid.c1].astype(F32)
            cgrad_ref[:, :, at_t * width + part * half : at_t * width + (part + 1) * half] = total.astype(
                BF16
            ).reshape(grid.bl, 2, half)

    def load_all(kv, carry):
        load_q(kv).start()
        load_g(kv).start()
        return carry

    run(load_all, 0, heads)
    block = jnp.int32(0)
    for i in range(order_ref.shape[0]):
        block = block + jnp.where(order_ref[i] == owner_ref[0], i, 0)
    mark[...] = jnp.full(mark.shape, block.astype(F32), F32)
    greet(grid)
    start_all(first_copy(0), grid.nu)
    start_all(mark_copy, grid.nb)
    start_all(first_copy(1), grid.nu)
    for part in range(2):
        first[part, in_plane] = cache[:, side(t, part)]
    marks[in_column] = mark[...]
    regroup[...] = shuffle(grid)
    pairing[...] = pairs()
    order = pairing[...]
    for j in range(TILES):
        split = dot_nn(order, kv_ref[j * ROWS : (j + 1) * ROWS].reshape(2 * ROWS, width)).astype(BF16)
        k_own[j * ROWS : (j + 1) * ROWS] = split[:ROWS]
        v_own[j * ROWS : (j + 1) * ROWS] = split[ROWS:]
    run(own_forward, 0, 2)
    wait_recv_all(mark_copy, grid.nb)
    many = grid.nu * grid.c1 // marks.shape[1]
    pick[...] = choice(
        grid, jnp.concatenate([marks[...]] * many, 1) if many > 1 else marks[:, : grid.nu * grid.c1]
    )
    send_rows(0)
    run(own_forward, 2, 3)
    send_rows(1)
    run(own_forward, 3, heads)
    take_rows(0)
    run(prompt_part, 0, heads // 2)
    send_terms(0)
    take_rows(1)
    run(prompt_part, heads // 2, heads)
    send_terms(1)
    run(own_backward, 0, 1)
    send_sums(0)
    run(own_backward, 1, 2)
    send_sums(1)
    run(own_backward, 2, heads)
    finish(0)
    finish(1)

    wait_send_all(mark_copy, grid.nb)
    for part in range(2):
        wait_send_all(first_copy(part), grid.nu)
        wait_send_all(second_copy(part), grid.nb)
        wait_send_all(third_copy(part), grid.nb)
        wait_send_all(fourth_copy(part), grid.nu)


def hand_on(*refs):
    copies = [pltpu.make_async_copy(refs[i], refs[4 + i], refs[8].at[i]) for i in range(4)]
    for copy in copies:
        copy.start()
    for copy in copies:
        copy.wait()


def local(
    grid,
    response_query,
    response_kv,
    prompt_cache,
    prompt_order,
    response_prompt,
    response_length,
    out_grad,
):
    width = response_kv.shape[3]
    heads = width // HD
    half = width // 2
    vmem = pl.BlockSpec(memory_space=pltpu.VMEM)
    smem = pl.BlockSpec(memory_space=pltpu.SMEM)
    hbm = pl.BlockSpec(memory_space=pl.ANY)
    dma = pltpu.SemaphoreType.DMA
    all_rows = grid.nb * grid.c2
    all_blocks = grid.nu * grid.c1
    full = (heads, RMAX, STACK)
    flat = response_query.shape[1:]
    out, dq, dkv, summed = pl.pallas_call(
        functools.partial(kernel, grid),
        out_shape=(
            jax.ShapeDtypeStruct(flat, BF16),
            jax.ShapeDtypeStruct(flat, BF16),
            jax.ShapeDtypeStruct((RMAX, 2, width), BF16),
            jax.ShapeDtypeStruct((grid.bl, 2, grid.nt * width), BF16),
        ),
        in_specs=[smem] * 3 + [vmem] * 2 + [hbm] * 2,
        out_specs=(vmem,) * 4,
        scratch_shapes=[
            pltpu.VMEM((all_rows, all_rows), BF16),
            pltpu.VMEM((2 * ROWS, 2 * ROWS), BF16),
            pltpu.VMEM((grid.c1, grid.nt * width), BF16),
            pltpu.VMEM((grid.c2, HD), F32),
            pltpu.VMEM((all_rows, HD), F32),
            pltpu.VMEM((2, all_blocks, half), BF16),
            pltpu.VMEM((all_rows, all_blocks), BF16),
            pltpu.VMEM((2, all_rows, half), BF16),
            pltpu.VMEM((2, all_rows, half), BF16),
            pltpu.VMEM((all_rows, width), BF16),
            pltpu.VMEM((all_rows, width), BF16),
            pltpu.VMEM((2, all_rows, half), BF16),
            pltpu.VMEM((2, all_rows, half), BF16),
            pltpu.VMEM((2, all_blocks, half), BF16),
            pltpu.VMEM((2, all_blocks, half), BF16),
            pltpu.VMEM(full, BF16),
            pltpu.VMEM(full, BF16),
            pltpu.VMEM((RMAX, width), BF16),
            pltpu.VMEM((RMAX, width), BF16),
            pltpu.VMEM((LOW, STACK), F32),
            pltpu.VMEM((heads, TILES, HD, STACK), BF16),
            pltpu.VMEM((heads, WIDE, STACK), BF16),
            pltpu.VMEM((heads, WIDE, STACK), F32),
            pltpu.VMEM((heads, TILES, 8, STACK), F32),
            pltpu.VMEM((heads, TILES, PLEN, STACK), BF16),
            pltpu.VMEM((heads, TILES, PLEN, STACK), BF16),
            pltpu.VMEM((LOW, STACK), BF16),
            pltpu.VMEM((LOW, STACK), BF16),
            pltpu.VMEM((RMAX, HD), F32),
            pltpu.VMEM((RMAX, HD), F32),
            dma((2, heads)),
            dma((grid.nb,)),
            dma((grid.nb,)),
            dma((2, grid.nu)),
            dma((2, grid.nu)),
            dma((2, grid.nb)),
            dma((2, grid.nb)),
            dma((2, grid.nb)),
            dma((2, grid.nb)),
            dma((2, grid.nu)),
            dma((2, grid.nu)),
        ],
        compiler_params=pltpu.CompilerParams(
            collective_id=0, has_side_effects=True, vmem_limit_bytes=46 * 1024 * 1024
        ),
    )(
        prompt_order,
        response_prompt,
        response_length,
        prompt_cache[0],
        response_kv[0],
        response_query[0],
        out_grad[0],
    )
    out, dq, dkv, summed = pl.pallas_call(
        hand_on,
        out_shape=tuple(jax.ShapeDtypeStruct(x.shape, x.dtype) for x in (out, dq, dkv, summed)),
        in_specs=[hbm] * 4,
        out_specs=(hbm,) * 4,
        scratch_shapes=[dma((4,))],
        compiler_params=pltpu.CompilerParams(vmem_limit_bytes=1024 * 1024),
    )(out, dq, dkv, summed)
    return (out[None], dq[None], dkv[None], summed[None])


def solution(mesh):
    grid = Grid(mesh.shape["seq"], mesh.shape["tp"], 16)
    return jax.shard_map(
        functools.partial(local, grid),
        mesh=mesh,
        in_specs=(
            P("seq", None, "tp"),
            P("seq", None, None, "tp"),
            P("seq", "tp", None, None),
            P(),
            P("seq"),
            P("seq"),
            P("seq", None, "tp"),
        ),
        out_specs=(
            P("seq", None, "tp"),
            P("seq", None, "tp"),
            P("seq", None, None, "tp"),
            P("seq", "tp", None, None),
        ),
        check_vma=False,
    )
```
